256 devices in a mesh: dp: 32 (over x, y, core), ctx: 8 (over z).
Axes of the slice: x: 4, y: 4, z: 8, core: 2. Of those that a mesh axis runs over, the one named last changes fastest.
Arguments:
- stream: bfloat16 [128, 7168], P('ctx', 'dp'), may hold values from -40 to 40
- query: bfloat16 [2, 64, 128, 576], P(None, 'dp'), may hold values from -80 to 80
- new_latent: bfloat16 [2, 64, 576], P(None, 'dp'), may hold values from -6 to 6
- cache: bfloat16 [64, 32768, 576], P('dp', 'ctx'), may hold values from -6 to 6
- cache_scale: float32 [64, 32768], P('dp', 'ctx'), may hold values from 0.25 to 2
- lengths: int32 [64], P('dp'), may hold values from 4096 to 32768, as said below
- absorb_value: bfloat16 [128, 512, 128], P('ctx'), may hold values from -6 to 6
- out_proj: bfloat16 [16384, 7168], P('ctx', 'dp'), may hold values from -0.046875 to 0.046875
- norm_gain: bfloat16 [7168], P('dp'), may hold values from 0.25 to 1.75
- gate_weight: bfloat16 [7168, 18432], P('dp', 'ctx'), may hold values from -0.0625 to 0.0625
- up_weight: bfloat16 [7168, 18432], P('dp', 'ctx'), may hold values from -0.0625 to 0.0625
- down_weight: bfloat16 [18432, 7168], P('ctx', 'dp'), may hold values from -0.375 to 0.375
Outputs:
- result: bfloat16 [128, 7168], P('ctx', 'dp')
The draws below stay inside these ranges and needn't reach their ends.
Inputs may be any that keep to these rules, and one draw needn't show every extreme that they name: `lengths`: every request holds at least 4096 cached positions and some request holds exactly 32768.
All inputs are finite; a program needn't handle non-finite values.
Results may differ from the reference program's by a relative error of at most 0.022.
Values may be sent and summed in bfloat16 or wider, within the bound.
No kernel may reach another device: no remote copies, remote signals or barrier semaphores. Data moves between devices by JAX's collectives and lax.ppermute only.
A program may use at most 64 MiB of HBM per device.

```python
import math
import jax
import jax.numpy as jnp
from jax import lax

D = 7168
FF = 18432
HEADS = 128
LATENT = 512
VHEAD = 128
QKHEAD = 192
STEPS = 2
KVW = 576
REQS = 64
CAP = 32768
TOKENS = 128


def anchor_rows(key):
    return jax.random.truncated_normal(jax.random.fold_in(key, 55), -6.0, 6.0, (REQS, KVW), jnp.float32)


def new_rows(key):
    return jax.random.truncated_normal(jax.random.fold_in(key, 77), -6.0, 6.0, (STEPS, REQS, KVW), jnp.float32)


def draw_new_latent(key, part):
    values = new_rows(key)
    return values.astype(jnp.bfloat16)


def draw_cache(key, part):
    anchors = anchor_rows(key)
    key = jax.random.fold_in(key, 3)
    values = jax.random.truncated_normal(key, -6.0, 6.0, (REQS, CAP, KVW), jnp.float32)
    first = jnp.arange(CAP)[None, :, None] == 0
    return jnp.where(first, anchors[:, None, :], values).astype(jnp.bfloat16)


def draw_query(key, part):
    key = jax.random.fold_in(key, 5)
    values = 0.5 * jax.random.truncated_normal(key, -6.0, 6.0, (STEPS, REQS, HEADS, KVW), jnp.float32)
    return values.astype(jnp.bfloat16)


def draw_lengths(key, part):
    key = jax.random.fold_in(key, 7)
    drawn = jax.random.randint(key, (REQS,), CAP // 8, CAP + 1, jnp.int32)
    chosen = jax.random.randint(jax.random.fold_in(key, 1), (), 0, REQS, jnp.int32)
    return jnp.where(jnp.arange(REQS, dtype=jnp.int32) == chosen, CAP, drawn).astype(jnp.int32)


def draw_stream(key, part):
    key = jax.random.fold_in(key, 9)
    column = 1.0 + 2.0 * jnp.arange(D, dtype=jnp.float32) / D
    values = jax.random.truncated_normal(key, -6.0, 6.0, (TOKENS, D), jnp.float32)
    return (values * column[None, :]).astype(jnp.bfloat16)


def levels(stream_key, extent, cuts, least, largest):
    level, own = 1.0, jax.random.fold_in(stream_key, 6)
    for axis_at, parts in cuts:
        draws = jnp.exp(jax.random.uniform(jax.random.fold_in(own, axis_at), (parts,), jnp.float32, least / len(cuts), largest / len(cuts)))
        level = level * jnp.repeat(draws, extent[axis_at] // parts).reshape([-1 if axis == axis_at else 1 for axis in range(len(extent))])
    return level


def noise(own_key, extent, deviation, reach, cuts=(), held_as=jnp.bfloat16):
    factor_of = levels(own_key, extent, cuts, -0.22, 0.18) if cuts else 1.0
    values = jax.random.normal(own_key, extent, jnp.float32) * deviation * factor_of
    return jnp.minimum(jnp.maximum(values, -reach), reach).astype(held_as)


def setup_inputs(seed: int = 0) -> dict:
    arg_keys = jax.random.split(jax.random.key(seed), 13)
    return {
        "stream": draw_stream(jax.random.fold_in(arg_keys[12], 71), 0),
        "query": draw_query(jax.random.fold_in(arg_keys[12], 71), 0),
        "new_latent": draw_new_latent(jax.random.fold_in(arg_keys[12], 71), 0),
        "cache": draw_cache(jax.random.fold_in(arg_keys[12], 71), 0),
        "cache_scale": jnp.clip(jnp.exp(math.log(2.0) - 2.0794415 * jax.random.uniform(arg_keys[4], (REQS, CAP), jnp.float32) ** levels(arg_keys[4], (REQS, CAP), ((0, 32), (1, 8)), -0.2, 0.2)), 0.25, 2.0),
        "lengths": draw_lengths(jax.random.fold_in(arg_keys[12], 71), 0),
        "absorb_value": noise(arg_keys[6], (HEADS, LATENT, VHEAD), 1.0, 6.0, ((0, 8),)),
        "out_proj": noise(arg_keys[7], (HEADS * VHEAD, D), (HEADS * VHEAD) ** -0.5, 0.046875, ((0, 8), (1, 32))),
        "norm_gain": jnp.clip(1.0 + 0.15 * jax.random.normal(arg_keys[8], (D,), jnp.float32), 0.25, 1.75).astype(jnp.bfloat16),
        "gate_weight": noise(arg_keys[9], (D, FF), D ** -0.5, 0.0625, ((0, 32), (1, 8))),
        "up_weight": noise(arg_keys[10], (D, FF), D ** -0.5, 0.0625, ((0, 32), (1, 8))),
        "down_weight": noise(arg_keys[11], (FF, D), (FF // 64) ** -0.5, 0.375, ((0, 8), (1, 32))),
    }


NEG = -1e+30
EPS = 1e-06

def attend_one(q_rows, cache_rows, scales, length, fresh):
    scale = QKHEAD ** (-0.5)
    rows = q_rows.shape[0]
    half = rows // 2
    old = jnp.dot(q_rows, cache_rows.T, preferred_element_type=jnp.float32) * scales[None, :] * scale
    valid = jnp.arange(CAP, dtype=jnp.int32)[None, :] < length
    new = jnp.dot(q_rows, fresh.T, preferred_element_type=jnp.float32) * scale
    new_ok = (jnp.arange(2, dtype=jnp.int32)[None, :] == 0) | (jnp.arange(rows, dtype=jnp.int32)[:, None] >= half)
    old = jnp.where(valid, old, NEG)
    new = jnp.where(new_ok, new, NEG)
    top = jnp.maximum(lax.optimization_barrier(jnp.max(old, axis=1)), lax.optimization_barrier(jnp.max(new, axis=1)))
    p_old = jnp.where(valid, jnp.exp(old - top[:, None]), 0.0)
    p_new = jnp.where(new_ok, jnp.exp(new - top[:, None]), 0.0)
    total = lax.optimization_barrier(jnp.sum(p_old, axis=1)) + lax.optimization_barrier(jnp.sum(p_new, axis=1))
    acc = jnp.dot((p_old * scales[None, :]).astype(jnp.bfloat16), cache_rows[:, :LATENT], preferred_element_type=jnp.float32)
    acc = acc + jnp.dot(p_new.astype(jnp.bfloat16), fresh[:, :LATENT], preferred_element_type=jnp.float32)
    return (acc / total[:, None]).astype(jnp.bfloat16)

def reference(stream, query, new_latent, cache, cache_scale, lengths, absorb_value, out_proj, norm_gain, gate_weight, up_weight, down_weight):
    q_rows = query.transpose(1, 0, 2, 3).reshape(REQS, STEPS * HEADS, KVW)
    fresh = new_latent.transpose(1, 0, 2)
    attended = lax.map(lambda a: attend_one(a[0], a[1], a[2], a[3], a[4]), (q_rows, cache, cache_scale, lengths, fresh))
    att4 = attended.reshape(REQS, STEPS, HEADS, LATENT)
    value = jnp.einsum('rshc,hcv->rshv', att4.astype(jnp.float32), absorb_value.astype(jnp.float32)).astype(jnp.bfloat16)
    flat = value.transpose(1, 0, 2, 3).reshape(TOKENS, HEADS * VHEAD)
    attn = jnp.dot(flat, out_proj, preferred_element_type=jnp.float32)
    mid = (stream.astype(jnp.float32) + attn).astype(jnp.bfloat16)
    mid32 = mid.astype(jnp.float32)
    meansq = lax.optimization_barrier(jnp.sum(mid32 * mid32, axis=1)) / D
    normed = (mid32 * lax.rsqrt(meansq + EPS)[:, None] * norm_gain.astype(jnp.float32)[None, :]).astype(jnp.bfloat16)
    gate = jnp.dot(normed, gate_weight, preferred_element_type=jnp.float32)
    up = jnp.dot(normed, up_weight, preferred_element_type=jnp.float32)
    hidden = (jax.nn.silu(gate) * up).astype(jnp.bfloat16)
    return (mid32 + jnp.dot(hidden, down_weight, preferred_element_type=jnp.float32)).astype(jnp.bfloat16)
```

```python
import functools

import jax
import jax.numpy as jnp
from jax import lax
from jax.experimental import pallas as pl
from jax.experimental.pallas import tpu as pltpu
from jax.sharding import PartitionSpec as P

D = 7168
LATENT = 512
QKHEAD = 192
EPS = 1e-06

SCORE = QKHEAD ** (-0.5) * 1.4426950408889634
NEG = -1e30
FLOOR = -1e29
META = 128
NT = (((1,), (1,)), ((), ()))
VMEM_BYTES = 56 * 2**20


def vmem(n):
    return [pl.BlockSpec(memory_space=pltpu.VMEM)] * n


def call(kernel, out_shape, in_specs, scratch=()):
    n_out = len(out_shape) if isinstance(out_shape, tuple) else 1
    out_specs = tuple(vmem(n_out)) if isinstance(out_shape, tuple) else vmem(1)[0]
    return pl.pallas_call(
        kernel,
        in_specs=in_specs,
        out_specs=out_specs,
        out_shape=out_shape,
        scratch_shapes=list(scratch),
        compiler_params=pltpu.CompilerParams(vmem_limit_bytes=VMEM_BYTES),
    )


def pieces(x):
    first = x.astype(jnp.bfloat16).astype(jnp.float32)
    rest = x - first
    second = rest.astype(jnp.bfloat16).astype(jnp.float32)
    return first, second, (rest - second).astype(jnp.bfloat16).astype(jnp.float32)


def in_lanes(columns, rows):
    lane = lax.broadcasted_iota(jnp.int32, (rows, META), 1)
    out = jnp.zeros((rows, META), jnp.float32)
    for i, column in enumerate(columns):
        out = jnp.where(lane == i, column, out)
    return out


def attend_kernel(
    where_ref, q_ref, new_ref, scale_ref, cache_ref, out_ref, keys, scores, sems, *, sub, cuts
):
    reqs, width, span = keys.shape
    groups = out_ref.shape[0]
    steps, heads = q_ref.shape[0], q_ref.shape[3]
    rows = steps * heads
    owned = heads // groups
    cut = span // cuts
    copies = [
        [
            pltpu.make_async_copy(
                cache_ref.at[r, :, pl.ds(i * cut, cut)],
                keys.at[r, :, pl.ds(i * cut, cut)],
                sems.at[r, i],
            )
            for i in range(cuts)
        ]
        for r in range(reqs)
    ]
    for r in range(reqs):
        for i in range(cuts):
            copies[r][i].start()

    def write(r, acc, top, total):
        meta = in_lanes(pieces(top) + pieces(total), rows).astype(jnp.bfloat16)
        acc = acc.astype(jnp.bfloat16)
        for s in range(steps):
            for g in range(groups):
                at = s * heads + g * owned
                out_ref[g, r, s, :, 0:LATENT] = acc[at : at + owned]
                out_ref[g, r, s, :, LATENT:] = meta[at : at + owned]

    for r in range(reqs):
        left = where_ref[r]

        @pl.when(left <= 0)
        def _():
            for i in range(cuts):
                copies[r][i].wait()
            write(
                r,
                jnp.zeros((rows, LATENT), jnp.float32),
                jnp.full((rows, 1), FLOOR, jnp.float32),
                jnp.zeros((rows, 1), jnp.float32),
            )

        @pl.when(left > 0)
        def _():
            q = jnp.concatenate([q_ref[s, r].T for s in range(steps)], axis=0)
            n = lax.broadcasted_iota(jnp.int32, (META, width), 0)
            fresh = jnp.zeros((META, width), jnp.float32)
            for s in range(steps):
                row = new_ref[s, r : r + 1, :].astype(jnp.float32)
                fresh = jnp.where(n == s, row, fresh)
            fresh = fresh.astype(jnp.bfloat16)
            new = lax.dot_general(q, fresh, NT, preferred_element_type=jnp.float32) * SCORE
            col = lax.broadcasted_iota(jnp.int32, (rows, META), 1)
            step = lax.broadcasted_iota(jnp.int32, (rows, META), 0) // heads
            new = jnp.where((col <= step) & (where_ref[reqs] == 0), new, NEG)
            top = jnp.maximum(new, FLOOR)
            for u in range(0, span, sub):
                if u % cut == 0:
                    copies[r][u // cut].wait()
                part = jnp.dot(q, keys[r, :, u : u + sub], preferred_element_type=jnp.float32)
                ok = lax.broadcasted_iota(jnp.int32, (1, sub), 1) + u < left
                factor = jnp.where(ok, scale_ref[r : r + 1, u : u + sub] * SCORE, 0.0)
                part = part * factor + jnp.where(ok, 0.0, NEG)
                scores[:, u : u + sub] = part
                for w in range(0, sub, META):
                    top = jnp.maximum(top, part[:, w : w + META])
            top = jnp.max(top, axis=1, keepdims=True)
            probs = jnp.exp2(new - top)
            total = probs
            acc = jnp.dot(
                probs.astype(jnp.bfloat16), fresh[:, :LATENT], preferred_element_type=jnp.float32
            )
            for u in range(0, span, sub):
                probs = jnp.exp2(scores[:, u : u + sub] - top)
                for w in range(0, sub, META):
                    total = total + probs[:, w : w + META]
                probs = (probs * scale_ref[r : r + 1, u : u + sub]).astype(jnp.bfloat16)
                acc = acc + lax.dot_general(
                    probs, keys[r, 0:LATENT, u : u + sub], NT, preferred_element_type=jnp.float32
                )
            write(r, acc, top, jnp.sum(total, axis=1, keepdims=True))


def value_kernel(part_ref, absorb_ref, out_ref):
    sources, rows, _ = part_ref.shape
    owned, _, vhead = absorb_ref.shape
    tokens = rows // owned
    half = owned // 2
    tops, totals = [], []
    for c in range(sources):
        meta = part_ref[c, :, LATENT:].astype(jnp.float32)
        tops.append(meta[:, 0:1] + meta[:, 1:2] + meta[:, 2:3])
        totals.append(meta[:, 3:4] + meta[:, 4:5] + meta[:, 5:6])
    top = functools.reduce(jnp.maximum, tops)
    total = jnp.zeros_like(top)
    acc = jnp.zeros((rows, LATENT), jnp.float32)
    for c in range(sources):
        factor = jnp.exp2(tops[c] - top)
        total = total + totals[c] * factor
        acc = acc + part_ref[c, :, :LATENT].astype(jnp.float32) * factor
    attended = (acc / total).astype(jnp.bfloat16)
    sides = []
    for side in range(2):
        cols = []
        for h in range(side * half, (side + 1) * half):
            each = jnp.dot(attended, absorb_ref[h], preferred_element_type=jnp.float32)
            cols.append(each.reshape(tokens, owned, vhead)[:, h, :])
        sides.append(jnp.concatenate(cols, axis=1))
    value = jnp.concatenate(sides, axis=0).astype(jnp.bfloat16)
    out_ref[...] = jnp.broadcast_to(value[None], out_ref.shape)


def project_kernel(value_ref, weight_ref, stream_ref, out_ref):
    holders, eight, half = value_ref.shape
    copies, _, cols = out_ref.shape
    tokens = holders * eight // 2
    x = value_ref[...].astype(jnp.float32).reshape(holders * eight, half).astype(jnp.bfloat16)
    low = lax.dot_general(x, weight_ref[:, :half], NT, preferred_element_type=jnp.float32)
    high = lax.dot_general(x, weight_ref[:, half:], NT, preferred_element_type=jnp.float32)
    both = low + jnp.concatenate([high[4:], high[:4]], axis=0)
    t = lax.broadcasted_iota(jnp.int32, (tokens, holders * eight), 0)
    k = lax.broadcasted_iota(jnp.int32, (tokens, holders * eight), 1)
    per = tokens // 2
    t_in = jnp.where(t >= per, t - per, t)
    source = 8 * (t_in // 2) + 2 * (t_in % 2) + jnp.where(t >= per, 1, 0)
    pick = jnp.where(k == source, 1.0, 0.0).astype(jnp.bfloat16)
    ordered = jnp.dot(
        pick, both.astype(jnp.bfloat16), preferred_element_type=jnp.float32
    ).astype(jnp.bfloat16)
    out_ref[:, :tokens, :] = jnp.broadcast_to(ordered[None], (copies, tokens, cols))
    stream = stream_ref[...]
    out_ref[:, tokens:, :] = jnp.broadcast_to(stream[None], (copies,) + stream.shape)


def gate_kernel(part_ref, gain_ref, gate_ref, up_ref, out_ref, mid_ref):
    sources, rows, cols = part_ref.shape
    owned = mid_ref.shape[0] // sources
    tokens = sources * owned
    chips, cores, eight, width = out_ref.shape
    half = gate_ref.shape[1] // cores
    attn = part_ref[0, :tokens, :].astype(jnp.float32)
    for c in range(1, sources):
        attn = attn + part_ref[c, :tokens, :].astype(jnp.float32)
    stream = jnp.concatenate(
        [part_ref[c, tokens:, :].astype(jnp.float32) for c in range(sources)], axis=0
    )
    mid = (stream + attn).astype(jnp.bfloat16)
    mid_ref[...] = mid
    mid = mid.astype(jnp.float32)
    squares = jnp.sum(mid * mid, axis=1, keepdims=True)
    meta = in_lanes(pieces(squares), tokens).reshape(chips, eight, META).astype(jnp.bfloat16)
    x = (mid * gain_ref[...].astype(jnp.float32)).astype(jnp.bfloat16)
    for k in range(cores):
        for i, weight in enumerate((gate_ref, up_ref)):
            y = jnp.dot(
                x, weight[:, k * half : (k + 1) * half], preferred_element_type=jnp.float32
            )
            out_ref[:, k, :, i * half : (i + 1) * half] = y.reshape(chips, eight, half).astype(
                jnp.bfloat16
            )
        out_ref[:, k, :, 2 * half :] = meta


def hidden_kernel(part_ref, out_ref):
    sources = part_ref.shape[0]
    half = out_ref.shape[2]
    both = part_ref[0].astype(jnp.float32)
    for d in range(1, sources):
        both = both + part_ref[d].astype(jnp.float32)
    squares = both[:, 2 * half : 2 * half + 1] + both[:, 2 * half + 1 : 2 * half + 2]
    squares = squares + both[:, 2 * half + 2 : 2 * half + 3]
    level = lax.rsqrt(squares / D + EPS)
    gate = both[:, :half] * level
    up = both[:, half : 2 * half] * level
    hidden = (gate / (1.0 + jnp.exp(-gate)) * up).astype(jnp.bfloat16)
    out_ref[...] = jnp.broadcast_to(hidden[None], out_ref.shape)


def down_kernel(hidden_ref, weight_ref, out_ref):
    chips, cores, eight, half = hidden_ref.shape
    total = None
    for k in range(cores):
        x = hidden_ref[:, k].astype(jnp.float32).reshape(chips * eight, half).astype(jnp.bfloat16)
        y = lax.dot_general(
            x, weight_ref[:, k * half : (k + 1) * half], NT, preferred_element_type=jnp.float32
        )
        total = y if total is None else total + y
    out_ref[...] = total.reshape(out_ref.shape).astype(jnp.bfloat16)


def finish_kernel(where_ref, part_ref, mid_ref, out_ref):
    sources, owned, _ = part_ref.shape
    total = mid_ref[pl.ds(pl.multiple_of(where_ref[0] * owned, owned), owned), :].astype(
        jnp.float32
    )
    ffn = part_ref[0].astype(jnp.float32)
    for c in range(1, sources):
        ffn = ffn + part_ref[c].astype(jnp.float32)
    out_ref[...] = (total + ffn).astype(jnp.bfloat16)


def exchange(x, axis):
    return lax.all_to_all(x, axis, 0, 0)


def on_device(
    stream,
    query,
    new_latent,
    cache,
    cache_scale,
    lengths,
    absorb_value,
    out_proj,
    norm_gain,
    gate_weight,
    up_weight,
    down_weight,
):
    steps, reqs, heads, width = query.shape
    span = cache.shape[1]
    groups = lax.axis_size("ctx")
    holders = lax.axis_size("dp")
    owned = heads // groups
    vhead = absorb_value.shape[2]
    cols = stream.shape[1]
    tokens = stream.shape[0] * groups
    units = gate_weight.shape[1]
    ctx_id = lax.axis_index("ctx").astype(jnp.int32)
    bf16 = jnp.bfloat16
    smem = pl.BlockSpec(memory_space=pltpu.SMEM)

    where = jnp.concatenate([lengths - ctx_id * span, ctx_id[None]])
    cuts = 4
    part = call(
        functools.partial(attend_kernel, sub=512, cuts=cuts),
        jax.ShapeDtypeStruct((groups, reqs, steps, owned, LATENT + META), bf16),
        [smem] + vmem(3) + [pl.BlockSpec(memory_space=pl.ANY)],
        [
            pltpu.VMEM((reqs, width, span), bf16),
            pltpu.VMEM((steps * heads, span), jnp.float32),
            pltpu.SemaphoreType.DMA((reqs, cuts)),
        ],
    )(where, query.transpose(0, 1, 3, 2), new_latent, cache_scale, cache.transpose(0, 2, 1))
    part = exchange(part.reshape(groups, reqs * steps * owned, LATENT + META), "ctx")

    value = call(
        value_kernel,
        jax.ShapeDtypeStruct((holders, 2 * steps * reqs, owned * vhead // 2), bf16),
        vmem(2),
    )(part, absorb_value)
    value = exchange(value, "dp")

    attn = call(
        project_kernel,
        jax.ShapeDtypeStruct((groups, tokens + stream.shape[0], cols), bf16),
        vmem(3),
    )(value, out_proj.T, stream)
    attn = exchange(attn, "ctx")

    both, mid = call(
        gate_kernel,
        (
            jax.ShapeDtypeStruct((holders // 2, 2, tokens * 2 // holders, units + META), bf16),
            jax.ShapeDtypeStruct((tokens, cols), bf16),
        ),
        vmem(4),
    )(attn, norm_gain.reshape(1, cols), gate_weight, up_weight)
    both = exchange(both.reshape(holders, tokens * 2 // holders, units + META), "dp")

    hidden = call(
        hidden_kernel,
        jax.ShapeDtypeStruct((holders, tokens * 2 // holders, units // 2), bf16),
        vmem(1),
    )(both)
    hidden = exchange(hidden, "dp")

    ffn = call(
        down_kernel,
        jax.ShapeDtypeStruct((groups, tokens // groups, cols), bf16),
        vmem(2),
    )(hidden.reshape(holders // 2, 2, tokens * 2 // holders, units // 2), down_weight.T)
    ffn = exchange(ffn, "ctx")

    return call(
        finish_kernel,
        jax.ShapeDtypeStruct(stream.shape, bf16),
        [smem] + vmem(2),
    )(ctx_id[None], ffn, mid)


def solution(mesh):
    return jax.shard_map(
        on_device,
        mesh=mesh,
        in_specs=(
            P("ctx", "dp"),
            P(None, "dp", None, None),
            P(None, "dp", None),
            P("dp", "ctx", None),
            P("dp", "ctx"),
            P("dp"),
            P("ctx", None, None),
            P("ctx", "dp"),
            P("dp"),
            P("dp", "ctx"),
            P("dp", "ctx"),
            P("ctx", "dp"),
        ),
        out_specs=P("ctx", "dp"),
        check_vma=False,
    )
```

```python
import functools

import jax
import jax.numpy as jnp
from jax import lax
from jax.experimental import pallas as pl
from jax.experimental.pallas import tpu as pltpu
from jax.sharding import PartitionSpec as P

D = 7168
LATENT = 512
QKHEAD = 192
EPS = 1e-06

SCORE = QKHEAD ** (-0.5) * 1.4426950408889634
NEG = -1e30
FLOOR = -1e29
META = 128
NT = (((1,), (1,)), ((), ()))


def vmem(n):
    return [pl.BlockSpec(memory_space=pltpu.VMEM)] * n


def call(kernel, out_shape, in_specs, scratch=(), mib=14):
    n_out = len(out_shape) if isinstance(out_shape, tuple) else 1
    out_specs = tuple(vmem(n_out)) if isinstance(out_shape, tuple) else vmem(1)[0]
    return pl.pallas_call(
        kernel,
        in_specs=in_specs,
        out_specs=out_specs,
        out_shape=out_shape,
        scratch_shapes=list(scratch),
        compiler_params=pltpu.CompilerParams(vmem_limit_bytes=mib * 2**20),
    )


def pieces(x):
    first = x.astype(jnp.bfloat16).astype(jnp.float32)
    rest = x - first
    second = rest.astype(jnp.bfloat16).astype(jnp.float32)
    return first, second, (rest - second).astype(jnp.bfloat16).astype(jnp.float32)


def in_lanes(columns, rows):
    lane = lax.broadcasted_iota(jnp.int32, (rows, META), 1)
    out = jnp.zeros((rows, META), jnp.float32)
    for i, column in enumerate(columns):
        out = jnp.where(lane == i, column, out)
    return out


def attend_kernel(
    lengths_ref, q_ref, new_ref, scale_ref, cache_ref, out_ref, keys, scores, sems, *, sub, cuts
):
    ctx_id = lax.axis_index("ctx")
    reqs, width, span = keys.shape
    groups = out_ref.shape[0]
    steps, heads = q_ref.shape[0], q_ref.shape[3]
    rows = steps * heads
    owned = heads // groups
    cut = span // cuts
    copies = [
        [
            pltpu.make_async_copy(
                cache_ref.at[r, :, pl.ds(i * cut, cut)],
                keys.at[r, :, pl.ds(i * cut, cut)],
                sems.at[r, i],
            )
            for i in range(cuts)
        ]
        for r in range(reqs)
    ]
    for r in range(reqs):
        for i in range(cuts):
            copies[r][i].start()

    def write(r, acc, top, total):
        acc = acc.astype(jnp.bfloat16)
        meta = in_lanes(pieces(top) + pieces(total), rows).T[:8].astype(jnp.bfloat16)
        for g in range(groups):
            for s in range(steps):
                at = s * heads + g * owned
                to = (r * steps + s) * owned
                out_ref[g, to : to + owned, :] = acc[at : at + owned]
            out_ref[g, reqs * steps * owned :, r * rows : (r + 1) * rows] = meta

    for r in range(reqs):
        left = lengths_ref[r] - ctx_id * span

        @pl.when(left <= 0)
        def _():
            for i in range(cuts):
                copies[r][i].wait()
            write(
                r,
                jnp.zeros((rows, LATENT), jnp.float32),
                jnp.full((rows, 1), FLOOR, jnp.float32),
                jnp.zeros((rows, 1), jnp.float32),
            )

        @pl.when(left > 0)
        def _():
            q = jnp.concatenate([q_ref[s, r].T for s in range(steps)], axis=0)
            n = lax.broadcasted_iota(jnp.int32, (META, width), 0)
            fresh = jnp.zeros((META, width), jnp.float32)
            for s in range(steps):
                row = new_ref[s, r : r + 1, :].astype(jnp.float32)
                fresh = jnp.where(n == s, row, fresh)
            fresh = fresh.astype(jnp.bfloat16)
            new = lax.dot_general(q, fresh, NT, preferred_element_type=jnp.float32) * SCORE
            col = lax.broadcasted_iota(jnp.int32, (rows, META), 1)
            step = lax.broadcasted_iota(jnp.int32, (rows, META), 0) // heads
            new = jnp.where((col <= step) & (ctx_id == 0), new, NEG)
            top = jnp.maximum(new, FLOOR)
            for u in range(0, span, sub):
                if u % cut == 0:
                    copies[r][u // cut].wait()
                part = jnp.dot(q, keys[r, :, u : u + sub], preferred_element_type=jnp.float32)
                ok = lax.broadcasted_iota(jnp.int32, (1, sub), 1) + u < left
                factor = jnp.where(ok, scale_ref[r : r + 1, u : u + sub] * SCORE, 0.0)
                part = part * factor + jnp.where(ok, 0.0, NEG)
                scores[:, u : u + sub] = part
                for w in range(0, sub, META):
                    top = jnp.maximum(top, part[:, w : w + META])
            top = jnp.max(top, axis=1, keepdims=True)
            probs = jnp.exp2(new - top)
            total = probs
            acc = jnp.dot(
                probs.astype(jnp.bfloat16), fresh[:, :LATENT], preferred_element_type=jnp.float32
            )
            for u in range(0, span, sub):
                probs = jnp.exp2(scores[:, u : u + sub] - top)
                for w in range(0, sub, META):
                    total = total + probs[:, w : w + META]
                probs = (probs * scale_ref[r : r + 1, u : u + sub]).astype(jnp.bfloat16)
                acc = acc + lax.dot_general(
                    probs, keys[r, 0:LATENT, u : u + sub], NT, preferred_element_type=jnp.float32
                )
            write(r, acc, top, jnp.sum(total, axis=1, keepdims=True))


def value_kernel(part_ref, absorb_ref, out_ref, marks):
    sources = part_ref.shape[0]
    owned, _, vhead = absorb_ref.shape
    reqs, all_rows, _ = marks.shape
    rows = part_ref.shape[1] - 8
    tokens = rows // owned
    steps = tokens // reqs
    heads = all_rows // steps
    half = owned // 2
    at = lax.axis_index("ctx") * owned
    found = []
    for r in range(reqs):
        meta = [part_ref[c, rows:, r * all_rows : (r + 1) * all_rows] for c in range(sources)]
        meta = jnp.concatenate([m.astype(jnp.float32) for m in meta], axis=0)
        marks[r] = meta.T
        for s in range(steps):
            found.append(marks[r, pl.ds(pl.multiple_of(s * heads + at, owned), owned), :])
    found = jnp.concatenate(found, axis=0)
    tops, totals = [], []
    for c in range(sources):
        i = 8 * c
        tops.append(found[:, i : i + 1] + found[:, i + 1 : i + 2] + found[:, i + 2 : i + 3])
        totals.append(found[:, i + 3 : i + 4] + found[:, i + 4 : i + 5] + found[:, i + 5 : i + 6])
    top = functools.reduce(jnp.maximum, tops)
    total = jnp.zeros_like(top)
    acc = jnp.zeros((rows, LATENT), jnp.float32)
    for c in range(sources):
        factor = jnp.exp2(tops[c] - top)
        total = total + totals[c] * factor
        acc = acc + part_ref[c, :rows, :].astype(jnp.float32) * factor
    attended = (acc / total).astype(jnp.bfloat16)
    sides = []
    for side in range(2):
        cols = []
        for h in range(side * half, (side + 1) * half):
            each = jnp.dot(attended, absorb_ref[h], preferred_element_type=jnp.float32)
            cols.append(each.reshape(tokens, owned, vhead)[:, h, :])
        sides.append(jnp.concatenate(cols, axis=1))
    value = jnp.concatenate(sides, axis=0).astype(jnp.bfloat16)
    out_ref[...] = jnp.broadcast_to(value[None], out_ref.shape)


def rows_of(x):
    x = x.astype(jnp.float32)
    return x.reshape(x.shape[0] * x.shape[1], x.shape[2]).astype(jnp.bfloat16)


def project_kernel(*refs):
    value_refs, (weight_ref, stream_ref, out_ref) = refs[:-3], refs[-3:]
    copies, cols, tokens = out_ref.shape
    owned = stream_ref.shape[0]
    per = tokens // 2
    x = jnp.concatenate([rows_of(ref[...]) for ref in value_refs], axis=0)
    half = x.shape[1]
    width = x.shape[0]
    low = lax.dot_general(weight_ref[:, :half], x, NT, preferred_element_type=jnp.float32)
    high = lax.dot_general(weight_ref[:, half:], x, NT, preferred_element_type=jnp.float32)
    both = low + pltpu.roll(high, width - 4, 1)

    def place(t):
        t_in = jnp.where(t >= per, t - per, t)
        d = t_in // 2
        if len(value_refs) == 2:
            core = lax.axis_index("dp") % 2
            first = jnp.where(d % 2 == core, 0, width // 2) + 8 * (d // 2)
        else:
            first = 8 * d
        return first + 2 * (t_in % 2) + jnp.where(t >= per, 1, 0)

    def one_hot(shape, token_dim, offset):
        t = lax.broadcasted_iota(jnp.int32, shape, token_dim) + offset
        k = lax.broadcasted_iota(jnp.int32, shape, 1 - token_dim)
        return jnp.where(k == place(t), 1.0, 0.0).astype(jnp.bfloat16)

    mine = one_hot((owned, width), 0, lax.axis_index("ctx") * owned)
    both = both + lax.dot_general(
        stream_ref[...], mine, (((0,), (0,)), ((), ())), preferred_element_type=jnp.float32
    )
    ordered = jnp.dot(
        both.astype(jnp.bfloat16),
        one_hot((width, tokens), 1, 0),
        preferred_element_type=jnp.float32,
    ).astype(jnp.bfloat16)
    out_ref[...] = jnp.broadcast_to(ordered[None], out_ref.shape)


def gate_kernel(part_ref, gain_ref, gate_ref, up_ref, send_ref, keep_ref, mid_ref, whole):
    sources, cols, tokens = part_ref.shape
    owned = mid_ref.shape[0]
    chips, eight, width = send_ref.shape
    half = gate_ref.shape[1] // 2
    mid = part_ref[0].astype(jnp.float32)
    for c in range(1, sources):
        mid = mid + part_ref[c].astype(jnp.float32)
    mid = mid.astype(jnp.bfloat16).astype(jnp.float32).T
    whole[...] = mid
    at = pl.multiple_of(lax.axis_index("ctx") * owned, owned)
    mid_ref[...] = whole[pl.ds(at, owned), :].astype(jnp.bfloat16)
    squares = pieces(jnp.sum(mid * mid, axis=1, keepdims=True))
    none = (jnp.zeros_like(squares[0]),) * 3
    x = (mid * gain_ref[...].astype(jnp.float32)).astype(jnp.bfloat16)
    core = lax.axis_index("dp") % 2
    for to_ref, k, marks in (
        (send_ref, 1 - core, squares),
        (keep_ref, core, none + squares),
    ):
        for i, weight in enumerate((gate_ref, up_ref)):
            columns = pl.ds(pl.multiple_of(k * half, META), half)
            y = jnp.dot(x, weight[:, columns], preferred_element_type=jnp.float32)
            to_ref[:, :, i * half : (i + 1) * half] = y.reshape(chips, eight, half).astype(
                to_ref.dtype
            )
        to_ref[:, :, 2 * half :] = (
            in_lanes(marks, tokens).reshape(chips, eight, META).astype(to_ref.dtype)
        )


def pair_kernel(keep_ref, got_ref, out_ref):
    out_ref[...] = (keep_ref[...] + got_ref[...].astype(jnp.float32)).astype(out_ref.dtype)


def hidden_kernel(part_ref, out_ref):
    sources = part_ref.shape[0]
    half = out_ref.shape[2]
    both = part_ref[0].astype(jnp.float32)
    for d in range(1, sources):
        both = both + part_ref[d].astype(jnp.float32)
    squares = jnp.sum(both[:, 2 * half :], axis=1, keepdims=True)
    level = lax.rsqrt(squares / D + EPS)
    gate = both[:, :half] * level
    up = both[:, half : 2 * half] * level
    hidden = (gate / (1.0 + jnp.exp(-gate)) * up).astype(jnp.bfloat16)
    out_ref[...] = jnp.broadcast_to(hidden[None], out_ref.shape)


def down_kernel(own_ref, other_ref, weight_ref, out_ref):
    half = own_ref.shape[2]
    core = lax.axis_index("dp") % 2
    total = None
    for ref, k in ((own_ref, core), (other_ref, 1 - core)):
        columns = pl.ds(pl.multiple_of(k * half, META), half)
        y = lax.dot_general(
            rows_of(ref[...]), weight_ref[:, columns], NT, preferred_element_type=jnp.float32
        )
        total = y if total is None else total + y
    out_ref[...] = total.reshape(out_ref.shape).astype(jnp.bfloat16)


def finish_kernel(part_ref, mid_ref, out_ref):
    ffn = part_ref[0].astype(jnp.float32)
    for c in range(1, part_ref.shape[0]):
        ffn = ffn + part_ref[c].astype(jnp.float32)
    out_ref[...] = (mid_ref[...].astype(jnp.float32) + ffn).astype(jnp.bfloat16)


def exchange(x, axis):
    return lax.all_to_all(x, axis, 0, 0)


def exchange_chips(x):
    size = lax.axis_size("dp")
    groups = [list(range(core, size, 2)) for core in range(2)]
    return lax.all_to_all(x, "dp", 0, 0, axis_index_groups=groups)


def other_core(x):
    return lax.ppermute(x, "dp", [(i, i ^ 1) for i in range(lax.axis_size("dp"))])


def on_device(
    stream,
    query,
    new_latent,
    cache,
    cache_scale,
    lengths,
    absorb_value,
    out_proj,
    norm_gain,
    gate_weight,
    up_weight,
    down_weight,
):
    steps, reqs, heads, width = query.shape
    span = cache.shape[1]
    groups = lax.axis_size("ctx")
    holders = lax.axis_size("dp")
    owned = heads // groups
    vhead = absorb_value.shape[2]
    cols = stream.shape[1]
    tokens = stream.shape[0] * groups
    units = gate_weight.shape[1]
    chips = holders // 2
    eight = 2 * steps * reqs
    bf16 = jnp.bfloat16
    f32 = jnp.float32
    smem = pl.BlockSpec(memory_space=pltpu.SMEM)

    cuts = 4
    part = call(
        functools.partial(attend_kernel, sub=512, cuts=cuts),
        jax.ShapeDtypeStruct((groups, reqs * steps * owned + 8, LATENT), bf16),
        [smem] + vmem(3) + [pl.BlockSpec(memory_space=pltpu.HBM)],
        [
            pltpu.VMEM((reqs, width, span), bf16),
            pltpu.VMEM((steps * heads, span), f32),
            pltpu.SemaphoreType.DMA((reqs, cuts)),
        ],
        mib=56,
    )(lengths, query.transpose(0, 1, 3, 2), new_latent, cache_scale, cache.transpose(0, 2, 1))
    part = exchange(part, "ctx")

    value = call(
        value_kernel,
        jax.ShapeDtypeStruct((chips, eight, owned * vhead // 2), bf16),
        vmem(2),
        [pltpu.VMEM((reqs, steps * heads, 8 * groups), f32)],
    )(part, absorb_value)
    value = exchange_chips(value)
    value = (value, other_core(value))

    attn = call(
        project_kernel,
        jax.ShapeDtypeStruct((groups, cols, tokens), bf16),
        vmem(len(value) + 2),
    )(*value, out_proj.T, stream)
    attn = exchange(attn, "ctx")

    block = (chips, tokens // chips, units + META)
    send, keep, mid = call(
        gate_kernel,
        (
            jax.ShapeDtypeStruct(block, bf16),
            jax.ShapeDtypeStruct(block, f32),
            jax.ShapeDtypeStruct(stream.shape, bf16),
        ),
        vmem(4),
        [pltpu.VMEM((tokens, cols), f32)],
    )(attn, norm_gain.reshape(1, cols), gate_weight, up_weight)
    both = call(pair_kernel, jax.ShapeDtypeStruct(block, bf16), vmem(2))(keep, other_core(send))
    both = exchange_chips(both)

    hidden = call(
        hidden_kernel,
        jax.ShapeDtypeStruct((chips, tokens // chips, units // 2), bf16),
        vmem(1),
    )(both)
    hidden = exchange_chips(hidden)

    ffn = call(
        down_kernel,
        jax.ShapeDtypeStruct((groups, tokens // groups, cols), bf16),
        vmem(3),
    )(hidden, other_core(hidden), down_weight.T)
    ffn = exchange(ffn, "ctx")

    return call(finish_kernel, jax.ShapeDtypeStruct(stream.shape, bf16), vmem(2))(ffn, mid)


def solution(mesh):
    return jax.shard_map(
        on_device,
        mesh=mesh,
        in_specs=(
            P("ctx", "dp"),
            P(None, "dp", None, None),
            P(None, "dp", None),
            P("dp", "ctx", None),
            P("dp", "ctx"),
            P("dp"),
            P("ctx", None, None),
            P("ctx", "dp"),
            P("dp"),
            P("dp", "ctx"),
            P("dp", "ctx"),
            P("ctx", "dp"),
        ),
        out_specs=P("ctx", "dp"),
        check_vma=False,
    )
```

```python
import functools

import jax
import jax.numpy as jnp
from jax import lax
from jax.experimental import pallas as pl
from jax.experimental.pallas import tpu as pltpu
from jax.sharding import PartitionSpec as P

D = 7168
LATENT = 512
QKHEAD = 192
EPS = 1e-06

SCORE = QKHEAD ** (-0.5) * 1.4426950408889634
NEG = -1e30
FLOOR = -1e29
META = 128
NT = (((1,), (1,)), ((), ()))


def vmem(n):
    return [pl.BlockSpec(memory_space=pltpu.VMEM)] * n


def call(kernel, out_shape, in_specs, scratch=(), mib=14, cost=None):
    n_out = len(out_shape) if isinstance(out_shape, tuple) else 1
    out_specs = tuple(vmem(n_out)) if isinstance(out_shape, tuple) else vmem(1)[0]
    return pl.pallas_call(
        kernel,
        in_specs=in_specs,
        out_specs=out_specs,
        out_shape=out_shape,
        scratch_shapes=list(scratch),
        compiler_params=pltpu.CompilerParams(vmem_limit_bytes=mib * 2**20),
        cost_estimate=cost,
    )


def pieces(x):
    first = x.astype(jnp.bfloat16).astype(jnp.float32)
    rest = x - first
    second = rest.astype(jnp.bfloat16).astype(jnp.float32)
    return first, second, (rest - second).astype(jnp.bfloat16).astype(jnp.float32)


def in_lanes(columns, rows):
    lane = lax.broadcasted_iota(jnp.int32, (rows, META), 1)
    out = jnp.zeros((rows, META), jnp.float32)
    for i, column in enumerate(columns):
        out = jnp.where(lane == i, column, out)
    return out


def attend_kernel(
    lengths_ref,
    q_hbm,
    new_hbm,
    scale_hbm,
    cache_hbm,
    out_ref,
    keys,
    scores,
    q_ref,
    new_ref,
    scale_ref,
    cache_sems,
    sems,
    *,
    sub,
    cuts,
):
    reqs, width, span = keys.shape
    groups = out_ref.shape[0]
    steps, heads = q_ref.shape[0], q_ref.shape[3]
    rows = steps * heads
    owned = heads // groups
    cut = span // cuts
    ctx_id = lax.axis_index("ctx")
    cache = [
        pltpu.make_async_copy(
            cache_hbm.at[r, :, pl.ds(i * cut, cut)],
            keys.at[r, :, pl.ds(i * cut, cut)],
            cache_sems.at[r, i],
        )
        for r in range(reqs)
        for i in range(cuts)
    ]
    small = [
        pltpu.make_async_copy(q_hbm, q_ref, sems.at[0]),
        pltpu.make_async_copy(new_hbm, new_ref, sems.at[1]),
        pltpu.make_async_copy(scale_hbm, scale_ref, sems.at[2]),
    ]
    small[0].start()
    cache[0].start()
    small[1].start()
    small[2].start()
    cache[1].start()
    for copy in small:
        copy.wait()

    def arrive(n):
        cache[n].wait()
        if n + 2 < len(cache):
            cache[n + 2].start()

    left = [lengths_ref[r] - ctx_id * span for r in range(reqs)]
    queries, fresh, new, tops, totals, sums = ([None] * reqs for _ in range(6))
    n = lax.broadcasted_iota(jnp.int32, (META, width), 0)
    col = lax.broadcasted_iota(jnp.int32, (rows, META), 1)
    step = lax.broadcasted_iota(jnp.int32, (rows, META), 0) // heads

    def begin(r):
        queries[r] = jnp.concatenate([q_ref[s, r].T for s in range(steps)], axis=0)
        tokens = jnp.zeros((META, width), jnp.float32)
        for s in range(steps):
            tokens = jnp.where(n == s, new_ref[s, r : r + 1, :].astype(jnp.float32), tokens)
        fresh[r] = tokens.astype(jnp.bfloat16)
        each = lax.dot_general(queries[r], fresh[r], NT, preferred_element_type=jnp.float32)
        new[r] = jnp.where((col <= step) & (ctx_id == 0), each * SCORE, NEG)
        tops[r] = jnp.maximum(new[r], FLOOR)

    def score(r, u):
        if u % cut == 0:
            arrive(r * cuts + u // cut)
        part = jnp.dot(queries[r], keys[r, :, u : u + sub], preferred_element_type=jnp.float32)
        ok = lax.broadcasted_iota(jnp.int32, (1, sub), 1) + u < left[r]
        factor = jnp.where(ok, scale_ref[r : r + 1, u : u + sub] * SCORE, 0.0)
        part = part * factor + jnp.where(ok, 0.0, NEG)
        scores[r, :, u : u + sub] = part
        for w in range(0, sub, META):
            tops[r] = jnp.maximum(tops[r], part[:, w : w + META])

    def top(r):
        tops[r] = jnp.max(tops[r], axis=1, keepdims=True)
        totals[r] = jnp.exp2(new[r] - tops[r])
        sums[r] = jnp.dot(
            totals[r].astype(jnp.bfloat16),
            fresh[r][:, :LATENT],
            preferred_element_type=jnp.float32,
        )

    def weigh(r, u):
        probs = jnp.exp2(scores[r, :, u : u + sub] - tops[r])
        for w in range(0, sub, META):
            totals[r] = totals[r] + probs[:, w : w + META]
        probs = (probs * scale_ref[r : r + 1, u : u + sub]).astype(jnp.bfloat16)
        sums[r] = sums[r] + lax.dot_general(
            probs, keys[r, 0:LATENT, u : u + sub], NT, preferred_element_type=jnp.float32
        )

    def write(r):
        acc = sums[r].astype(jnp.bfloat16)
        total = jnp.sum(totals[r], axis=1, keepdims=True)
        meta = in_lanes(pieces(tops[r]) + pieces(total), rows).T[:8].astype(jnp.bfloat16)
        for g in range(groups):
            for s in range(steps):
                at = s * heads + g * owned
                to = (r * steps + s) * owned
                out_ref[g, to : to + owned, :] = acc[at : at + owned]
            out_ref[g, reqs * steps * owned :, r * rows : (r + 1) * rows] = meta

    for r in range(reqs):
        begin(r)
    for r in range(reqs + 1):
        for u in range(0, span, sub):
            if r < reqs:
                score(r, u)
            if r > 0:
                weigh(r - 1, u)
        if r > 0:
            write(r - 1)
        if r < reqs:
            top(r)


def value_kernel(part_ref, absorb_ref, out_ref, marks):
    sources = part_ref.shape[0]
    owned, _, vhead = absorb_ref.shape
    reqs, all_rows, _ = marks.shape
    rows = part_ref.shape[1] - 8
    tokens = rows // owned
    steps = tokens // reqs
    heads = all_rows // steps
    half = owned // 2
    at = lax.axis_index("ctx") * owned
    found = []
    for r in range(reqs):
        meta = [part_ref[c, rows:, r * all_rows : (r + 1) * all_rows] for c in range(sources)]
        meta = jnp.concatenate([m.astype(jnp.float32) for m in meta], axis=0)
        marks[r] = meta.T
        for s in range(steps):
            found.append(marks[r, pl.ds(pl.multiple_of(s * heads + at, owned), owned), :])
    found = jnp.concatenate(found, axis=0)
    tops, totals = [], []
    for c in range(sources):
        i = 8 * c
        tops.append(found[:, i : i + 1] + found[:, i + 1 : i + 2] + found[:, i + 2 : i + 3])
        totals.append(found[:, i + 3 : i + 4] + found[:, i + 4 : i + 5] + found[:, i + 5 : i + 6])
    top = functools.reduce(jnp.maximum, tops)
    total = jnp.zeros_like(top)
    acc = jnp.zeros((rows, LATENT), jnp.float32)
    for c in range(sources):
        factor = jnp.exp2(tops[c] - top)
        total = total + totals[c] * factor
        acc = acc + part_ref[c, :rows, :].astype(jnp.float32) * factor
    attended = (acc / total).astype(jnp.bfloat16)
    sides = []
    for side in range(2):
        cols = []
        for h in range(side * half, (side + 1) * half):
            each = jnp.dot(attended, absorb_ref[h], preferred_element_type=jnp.float32)
            cols.append(each.reshape(tokens, owned, vhead)[:, h, :])
        sides.append(jnp.concatenate(cols, axis=1))
    value = jnp.concatenate(sides, axis=0).astype(jnp.bfloat16)
    out_ref[...] = jnp.broadcast_to(value[None], out_ref.shape)


def rows_of(x):
    x = x.astype(jnp.float32)
    return x.reshape(x.shape[0] * x.shape[1], x.shape[2]).astype(jnp.bfloat16)


def product(value_ref, weight_ref):
    x = rows_of(value_ref[...])
    half = x.shape[1]
    low = lax.dot_general(weight_ref[:, :half], x, NT, preferred_element_type=jnp.float32)
    high = lax.dot_general(weight_ref[:, half:], x, NT, preferred_element_type=jnp.float32)
    return low + pltpu.roll(high, x.shape[0] - 4, 1)


def product_kernel(value_ref, weight_ref, out_ref):
    out_ref[...] = product(value_ref, weight_ref)


def project_kernel(own_ref, value_ref, weight_ref, stream_ref, out_ref):
    copies, cols, tokens = out_ref.shape
    owned = stream_ref.shape[0]
    per = tokens // 2
    width = 2 * own_ref.shape[1]
    core = lax.axis_index("dp") % 2

    def place(t):
        t_in = jnp.where(t >= per, t - per, t)
        d = t_in // 2
        first = jnp.where(d % 2 == core, 0, width // 2) + 8 * (d // 2)
        return first + 2 * (t_in % 2) + jnp.where(t >= per, 1, 0)

    def one_hot(shape, token_dim, offset):
        t = lax.broadcasted_iota(jnp.int32, shape, token_dim) + offset
        k = lax.broadcasted_iota(jnp.int32, shape, 1 - token_dim)
        return jnp.where(k == place(t), 1.0, 0.0).astype(jnp.bfloat16)

    both = jnp.concatenate([own_ref[...], product(value_ref, weight_ref)], axis=1)
    mine = one_hot((owned, width), 0, lax.axis_index("ctx") * owned)
    both = both + lax.dot_general(
        stream_ref[...], mine, (((0,), (0,)), ((), ())), preferred_element_type=jnp.float32
    )
    ordered = jnp.dot(
        both.astype(jnp.bfloat16),
        one_hot((width, tokens), 1, 0),
        preferred_element_type=jnp.float32,
    ).astype(jnp.bfloat16)
    out_ref[...] = jnp.broadcast_to(ordered[None], out_ref.shape)


def gate_kernel(part_ref, gain_ref, gate_ref, up_ref, send_ref, keep_ref, mid_ref, whole):
    sources, cols, tokens = part_ref.shape
    owned = mid_ref.shape[0]
    chips, eight, width = send_ref.shape
    half = gate_ref.shape[1] // 2
    mid = part_ref[0].astype(jnp.float32)
    for c in range(1, sources):
        mid = mid + part_ref[c].astype(jnp.float32)
    mid = mid.astype(jnp.bfloat16).astype(jnp.float32).T
    whole[...] = mid
    at = pl.multiple_of(lax.axis_index("ctx") * owned, owned)
    mid_ref[...] = whole[pl.ds(at, owned), :].astype(jnp.bfloat16)
    squares = pieces(jnp.sum(mid * mid, axis=1, keepdims=True))
    none = (jnp.zeros_like(squares[0]),) * 3
    x = (mid * gain_ref[...].astype(jnp.float32)).astype(jnp.bfloat16)
    core = lax.axis_index("dp") % 2
    for to_ref, k, marks in (
        (send_ref, 1 - core, squares),
        (keep_ref, core, none + squares),
    ):
        for i, weight in enumerate((gate_ref, up_ref)):
            columns = pl.ds(pl.multiple_of(k * half, META), half)
            y = jnp.dot(x, weight[:, columns], preferred_element_type=jnp.float32)
            to_ref[:, :, i * half : (i + 1) * half] = y.reshape(chips, eight, half).astype(
                to_ref.dtype
            )
        to_ref[:, :, 2 * half :] = (
            in_lanes(marks, tokens).reshape(chips, eight, META).astype(to_ref.dtype)
        )


def pair_kernel(keep_ref, got_ref, out_ref):
    out_ref[...] = (keep_ref[...] + got_ref[...].astype(jnp.float32)).astype(out_ref.dtype)


def hidden_kernel(part_ref, out_ref):
    sources = part_ref.shape[0]
    half = out_ref.shape[2]
    both = part_ref[0].astype(jnp.float32)
    for d in range(1, sources):
        both = both + part_ref[d].astype(jnp.float32)
    squares = jnp.sum(both[:, 2 * half :], axis=1, keepdims=True)
    level = lax.rsqrt(squares / D + EPS)
    gate = both[:, :half] * level
    up = both[:, half : 2 * half] * level
    hidden = (gate / (1.0 + jnp.exp(-gate)) * up).astype(jnp.bfloat16)
    out_ref[...] = jnp.broadcast_to(hidden[None], out_ref.shape)


def down(hidden_ref, weight_ref, k):
    half = hidden_ref.shape[2]
    columns = pl.ds(pl.multiple_of(k * half, META), half)
    return lax.dot_general(
        rows_of(hidden_ref[...]),
        weight_ref[:, columns],
        NT,
        preferred_element_type=jnp.float32,
    )


def down_own_kernel(hidden_ref, weight_ref, out_ref):
    out_ref[...] = down(hidden_ref, weight_ref, lax.axis_index("dp") % 2)


def down_kernel(own_ref, hidden_ref, weight_ref, out_ref):
    total = own_ref[...] + down(hidden_ref, weight_ref, 1 - lax.axis_index("dp") % 2)
    out_ref[...] = total.reshape(out_ref.shape).astype(jnp.bfloat16)


def finish_kernel(part_ref, mid_ref, out_ref):
    ffn = part_ref[0].astype(jnp.float32)
    for c in range(1, part_ref.shape[0]):
        ffn = ffn + part_ref[c].astype(jnp.float32)
    out_ref[...] = (mid_ref[...].astype(jnp.float32) + ffn).astype(jnp.bfloat16)


def exchange(x, axis):
    return lax.all_to_all(x, axis, 0, 0)


def exchange_chips(x):
    size = lax.axis_size("dp")
    groups = [list(range(core, size, 2)) for core in range(2)]
    return lax.all_to_all(x, "dp", 0, 0, axis_index_groups=groups)


def other_core(x):
    return lax.ppermute(x, "dp", [(i, i ^ 1) for i in range(lax.axis_size("dp"))])


def on_device(
    stream,
    query,
    new_latent,
    cache,
    cache_scale,
    lengths,
    absorb_value,
    out_proj,
    norm_gain,
    gate_weight,
    up_weight,
    down_weight,
):
    steps, reqs, heads, width = query.shape
    span = cache.shape[1]
    groups = lax.axis_size("ctx")
    holders = lax.axis_size("dp")
    owned = heads // groups
    vhead = absorb_value.shape[2]
    cols = stream.shape[1]
    tokens = stream.shape[0] * groups
    units = gate_weight.shape[1]
    chips = holders // 2
    eight = 2 * steps * reqs
    bf16 = jnp.bfloat16
    f32 = jnp.float32
    smem = pl.BlockSpec(memory_space=pltpu.SMEM)

    cuts = 2
    part = call(
        functools.partial(attend_kernel, sub=512, cuts=cuts),
        jax.ShapeDtypeStruct((groups, reqs * steps * owned + 8, LATENT), bf16),
        [smem] + [pl.BlockSpec(memory_space=pltpu.HBM)] * 4,
        [
            pltpu.VMEM((reqs, width, span), bf16),
            pltpu.VMEM((reqs, steps * heads, span), f32),
            pltpu.VMEM((steps, reqs, width, heads), bf16),
            pltpu.VMEM((steps, reqs, width), bf16),
            pltpu.VMEM((reqs, span), f32),
            pltpu.SemaphoreType.DMA((reqs, cuts)),
            pltpu.SemaphoreType.DMA((3,)),
        ],
        mib=56,
    )(lengths, query.transpose(0, 1, 3, 2), new_latent, cache_scale, cache.transpose(0, 2, 1))
    part = exchange(part, "ctx")

    value = call(
        value_kernel,
        jax.ShapeDtypeStruct((chips, eight, owned * vhead // 2), bf16),
        vmem(2),
        [pltpu.VMEM((reqs, steps * heads, 8 * groups), f32)],
    )(part, absorb_value)
    value = exchange_chips(value)
    other = other_core(value)
    work = pl.CostEstimate(flops=2**29, bytes_accessed=2**20, transcendentals=0)
    attn = call(
        product_kernel,
        jax.ShapeDtypeStruct((cols, chips * eight), f32),
        vmem(2),
        cost=work,
    )(value, out_proj.T)
    attn = call(
        project_kernel,
        jax.ShapeDtypeStruct((groups, cols, tokens), bf16),
        vmem(4),
    )(attn, other, out_proj.T, stream)
    attn = exchange(attn, "ctx")

    block = (chips, tokens // chips, units + META)
    send, keep, mid = call(
        gate_kernel,
        (
            jax.ShapeDtypeStruct(block, bf16),
            jax.ShapeDtypeStruct(block, f32),
            jax.ShapeDtypeStruct(stream.shape, bf16),
        ),
        vmem(4),
        [pltpu.VMEM((tokens, cols), f32)],
    )(attn, norm_gain.reshape(1, cols), gate_weight, up_weight)
    both = call(pair_kernel, jax.ShapeDtypeStruct(block, bf16), vmem(2))(keep, other_core(send))
    both = exchange_chips(both)

    hidden = call(
        hidden_kernel,
        jax.ShapeDtypeStruct((chips, tokens // chips, units // 2), bf16),
        vmem(1),
    )(both)
    hidden = exchange_chips(hidden)

    other = other_core(hidden)
    ffn = call(
        down_own_kernel,
        jax.ShapeDtypeStruct((tokens, cols), f32),
        vmem(2),
        cost=work,
    )(hidden, down_weight.T)
    ffn = call(
        down_kernel,
        jax.ShapeDtypeStruct((groups, tokens // groups, cols), bf16),
        vmem(3),
    )(ffn, other, down_weight.T)
    ffn = exchange(ffn, "ctx")

    return call(finish_kernel, jax.ShapeDtypeStruct(stream.shape, bf16), vmem(2))(ffn, mid)


def solution(mesh):
    return jax.shard_map(
        on_device,
        mesh=mesh,
        in_specs=(
            P("ctx", "dp"),
            P(None, "dp", None, None),
            P(None, "dp", None),
            P("dp", "ctx", None),
            P("dp", "ctx"),
            P("dp"),
            P("ctx", None, None),
            P("ctx", "dp"),
            P("dp"),
            P("dp", "ctx"),
            P("dp", "ctx"),
            P("ctx", "dp"),
        ),
        out_specs=P("ctx", "dp"),
        check_vma=False,
    )
```

```python
import functools

import jax
import jax.numpy as jnp
from jax import lax
from jax.experimental import pallas as pl
from jax.experimental.pallas import tpu as pltpu
from jax.sharding import PartitionSpec as P

D = 7168
LATENT = 512
QKHEAD = 192
EPS = 1e-06

SCORE = QKHEAD ** (-0.5) * 1.4426950408889634
NEG = -1e30
FLOOR = -1e29
META = 128
NT = (((1,), (1,)), ((), ()))


def vmem(n):
    return [pl.BlockSpec(memory_space=pltpu.VMEM)] * n


def call(kernel, out_shape, in_specs, scratch=(), mib=14, cost=None):
    n_out = len(out_shape) if isinstance(out_shape, tuple) else 1
    out_specs = tuple(vmem(n_out)) if isinstance(out_shape, tuple) else vmem(1)[0]
    return pl.pallas_call(
        kernel,
        in_specs=in_specs,
        out_specs=out_specs,
        out_shape=out_shape,
        scratch_shapes=list(scratch),
        compiler_params=pltpu.CompilerParams(vmem_limit_bytes=mib * 2**20),
        cost_estimate=cost,
    )


def pieces(x):
    first = x.astype(jnp.bfloat16).astype(jnp.float32)
    rest = x - first
    second = rest.astype(jnp.bfloat16).astype(jnp.float32)
    return first, second, (rest - second).astype(jnp.bfloat16).astype(jnp.float32)


def in_lanes(columns, rows):
    lane = lax.broadcasted_iota(jnp.int32, (rows, META), 1)
    out = jnp.zeros((rows, META), jnp.float32)
    for i, column in enumerate(columns):
        out = jnp.where(lane == i, column, out)
    return out


def attend_kernel(
    lengths_ref,
    q_hbm,
    new_hbm,
    scale_hbm,
    cache_hbm,
    out_ref,
    keys,
    scores,
    q_ref,
    new_ref,
    scale_ref,
    cache_sems,
    sems,
    *,
    sub,
    cuts,
):
    reqs, width, span = keys.shape
    groups = out_ref.shape[0]
    steps, heads = q_ref.shape[0], q_ref.shape[3]
    rows = steps * heads
    owned = heads // groups
    cut = span // cuts
    ctx_id = lax.axis_index("ctx")
    cache = [
        pltpu.make_async_copy(
            cache_hbm.at[r, :, pl.ds(i * cut, cut)],
            keys.at[r, :, pl.ds(i * cut, cut)],
            cache_sems.at[r, i],
        )
        for r in range(reqs)
        for i in range(cuts)
    ]
    small = [
        pltpu.make_async_copy(q_hbm, q_ref, sems.at[0]),
        pltpu.make_async_copy(new_hbm, new_ref, sems.at[1]),
        pltpu.make_async_copy(scale_hbm, scale_ref, sems.at[2]),
    ]

    left = [lengths_ref[r] - ctx_id * span for r in range(reqs)]
    queries, fresh, new, tops, totals, sums = ([None] * reqs for _ in range(6))
    n = lax.broadcasted_iota(jnp.int32, (META, width), 0)
    col = lax.broadcasted_iota(jnp.int32, (rows, META), 1)
    step = lax.broadcasted_iota(jnp.int32, (rows, META), 0) // heads

    def begin(r):
        queries[r] = jnp.concatenate([q_ref[s, r].T for s in range(steps)], axis=0)
        tokens = jnp.zeros((META, width), jnp.float32)
        for s in range(steps):
            tokens = jnp.where(n == s, new_ref[s, r : r + 1, :].astype(jnp.float32), tokens)
        fresh[r] = tokens.astype(jnp.bfloat16)
        each = lax.dot_general(queries[r], fresh[r], NT, preferred_element_type=jnp.float32)
        new[r] = jnp.where((col <= step) & (ctx_id == 0), each * SCORE, NEG)
        tops[r] = jnp.maximum(new[r], FLOOR)

    def score(r, u):
        part = jnp.dot(queries[r], keys[r, :, u : u + sub], preferred_element_type=jnp.float32)
        ok = lax.broadcasted_iota(jnp.int32, (1, sub), 1) + u < left[r]
        factor = jnp.where(ok, scale_ref[r : r + 1, u : u + sub] * SCORE, 0.0)
        part = part * factor + jnp.where(ok, 0.0, NEG)
        scores[r, :, u : u + sub] = part
        for w in range(0, sub, META):
            tops[r] = jnp.maximum(tops[r], part[:, w : w + META])

    def top(r):
        tops[r] = jnp.max(tops[r], axis=1, keepdims=True)
        totals[r] = jnp.exp2(new[r] - tops[r])
        sums[r] = jnp.dot(
            totals[r].astype(jnp.bfloat16),
            fresh[r][:, :LATENT],
            preferred_element_type=jnp.float32,
        )

    def weigh(r, u):
        probs = jnp.exp2(scores[r, :, u : u + sub] - tops[r])
        for w in range(0, sub, META):
            totals[r] = totals[r] + probs[:, w : w + META]
        probs = (probs * scale_ref[r : r + 1, u : u + sub]).astype(jnp.bfloat16)
        sums[r] = sums[r] + lax.dot_general(
            probs, keys[r, 0:LATENT, u : u + sub], NT, preferred_element_type=jnp.float32
        )

    def write(r):
        acc = sums[r].astype(jnp.bfloat16)
        total = jnp.sum(totals[r], axis=1, keepdims=True)
        meta = in_lanes(pieces(tops[r]) + pieces(total), rows).T[:8].astype(jnp.bfloat16)
        for g in range(groups):
            for s in range(steps):
                at = s * heads + g * owned
                to = (r * steps + s) * owned
                out_ref[g, to : to + owned, :] = acc[at : at + owned]
            out_ref[g, reqs * steps * owned :, r * rows : (r + 1) * rows] = meta

    def attend(active):
        order = [r * cuts + i for r in active for i in range(cuts)]
        small[0].start()
        cache[order[0]].start()
        small[1].start()
        small[2].start()
        cache[order[1]].start()
        for copy in small:
            copy.wait()
        for r in active:
            begin(r)
        for n in range(len(active) + 1):
            for u in range(0, span, sub):
                if n < len(active):
                    if u % cut == 0:
                        at = n * cuts + u // cut
                        cache[order[at]].wait()
                        if at + 2 < len(order):
                            cache[order[at + 2]].start()
                    score(active[n], u)
                if n > 0:
                    weigh(active[n - 1], u)
            if n > 0:
                write(active[n - 1])
            if n < len(active):
                top(active[n])
        for r in range(reqs):
            if r not in active:
                skip(r)

    def skip(r):
        tops[r] = jnp.full((rows, 1), FLOOR, jnp.float32)
        totals[r] = jnp.zeros((rows, 1), jnp.float32)
        sums[r] = jnp.zeros((rows, LATENT), jnp.float32)
        write(r)

    first, second = (left[r] > 0 for r in range(reqs))

    @pl.when(first & second)
    def _():
        attend([0, 1])

    @pl.when(first & ~second)
    def _():
        attend([0])

    @pl.when(second & ~first)
    def _():
        attend([1])

    @pl.when(~first & ~second)
    def _():
        for r in range(reqs):
            skip(r)


def value_kernel(part_ref, absorb_ref, out_ref, marks):
    sources = part_ref.shape[0]
    owned, _, vhead = absorb_ref.shape
    reqs, all_rows, _ = marks.shape
    rows = part_ref.shape[1] - 8
    tokens = rows // owned
    steps = tokens // reqs
    heads = all_rows // steps
    half = owned // 2
    at = lax.axis_index("ctx") * owned
    found = []
    for r in range(reqs):
        meta = [part_ref[c, rows:, r * all_rows : (r + 1) * all_rows] for c in range(sources)]
        meta = jnp.concatenate([m.astype(jnp.float32) for m in meta], axis=0)
        marks[r] = meta.T
        for s in range(steps):
            found.append(marks[r, pl.ds(pl.multiple_of(s * heads + at, owned), owned), :])
    found = jnp.concatenate(found, axis=0)
    tops, totals = [], []
    for c in range(sources):
        i = 8 * c
        tops.append(found[:, i : i + 1] + found[:, i + 1 : i + 2] + found[:, i + 2 : i + 3])
        totals.append(found[:, i + 3 : i + 4] + found[:, i + 4 : i + 5] + found[:, i + 5 : i + 6])
    top = functools.reduce(jnp.maximum, tops)
    total = jnp.zeros_like(top)
    acc = jnp.zeros((rows, LATENT), jnp.float32)
    for c in range(sources):
        factor = jnp.exp2(tops[c] - top)
        total = total + totals[c] * factor
        acc = acc + part_ref[c, :rows, :].astype(jnp.float32) * factor
    attended = (acc / total).astype(jnp.bfloat16)
    sides = []
    for side in range(2):
        cols = []
        for h in range(side * half, (side + 1) * half):
            each = jnp.dot(attended, absorb_ref[h], preferred_element_type=jnp.float32)
            cols.append(each.reshape(tokens, owned, vhead)[:, h, :])
        sides.append(jnp.concatenate(cols, axis=1))
    value = jnp.concatenate(sides, axis=0).astype(jnp.bfloat16)
    out_ref[...] = jnp.broadcast_to(value[None], out_ref.shape)


def rows_of(x):
    x = x.astype(jnp.float32)
    return x.reshape(x.shape[0] * x.shape[1], x.shape[2]).astype(jnp.bfloat16)


def product(value_ref, weight_ref):
    x = rows_of(value_ref[...])
    half = x.shape[1]
    low = lax.dot_general(weight_ref[:, :half], x, NT, preferred_element_type=jnp.float32)
    high = lax.dot_general(weight_ref[:, half:], x, NT, preferred_element_type=jnp.float32)
    return low + pltpu.roll(high, x.shape[0] - 4, 1)


def product_kernel(value_ref, weight_ref, out_ref):
    out_ref[...] = product(value_ref, weight_ref)


def project_kernel(own_ref, value_ref, weight_ref, stream_ref, out_ref):
    copies, cols, tokens = out_ref.shape
    owned = stream_ref.shape[0]
    per = tokens // 2
    width = 2 * own_ref.shape[1]
    core = lax.axis_index("dp") % 2

    def place(t):
        t_in = jnp.where(t >= per, t - per, t)
        d = t_in // 2
        first = jnp.where(d % 2 == core, 0, width // 2) + 8 * (d // 2)
        return first + 2 * (t_in % 2) + jnp.where(t >= per, 1, 0)

    def one_hot(shape, token_dim, offset):
        t = lax.broadcasted_iota(jnp.int32, shape, token_dim) + offset
        k = lax.broadcasted_iota(jnp.int32, shape, 1 - token_dim)
        return jnp.where(k == place(t), 1.0, 0.0).astype(jnp.bfloat16)

    both = jnp.concatenate([own_ref[...], product(value_ref, weight_ref)], axis=1)
    mine = one_hot((owned, width), 0, lax.axis_index("ctx") * owned)
    both = both + lax.dot_general(
        stream_ref[...], mine, (((0,), (0,)), ((), ())), preferred_element_type=jnp.float32
    )
    ordered = jnp.dot(
        both.astype(jnp.bfloat16),
        one_hot((width, tokens), 1, 0),
        preferred_element_type=jnp.float32,
    ).astype(jnp.bfloat16)
    out_ref[...] = jnp.broadcast_to(ordered[None], out_ref.shape)


def gate_kernel(part_ref, gain_ref, gate_ref, up_ref, send_ref, keep_ref, mid_ref, whole):
    sources, cols, tokens = part_ref.shape
    owned = mid_ref.shape[0]
    chips, eight, width = send_ref.shape
    half = gate_ref.shape[1] // 2
    mid = part_ref[0].astype(jnp.float32)
    for c in range(1, sources):
        mid = mid + part_ref[c].astype(jnp.float32)
    mid = mid.astype(jnp.bfloat16).astype(jnp.float32).T
    whole[...] = mid
    at = pl.multiple_of(lax.axis_index("ctx") * owned, owned)
    mid_ref[...] = whole[pl.ds(at, owned), :].astype(jnp.bfloat16)
    squares = pieces(jnp.sum(mid * mid, axis=1, keepdims=True))
    none = (jnp.zeros_like(squares[0]),) * 3
    x = (mid * gain_ref[...].astype(jnp.float32)).astype(jnp.bfloat16)
    core = lax.axis_index("dp") % 2
    for to_ref, k, marks in (
        (send_ref, 1 - core, squares),
        (keep_ref, core, none + squares),
    ):
        for i, weight in enumerate((gate_ref, up_ref)):
            columns = pl.ds(pl.multiple_of(k * half, META), half)
            y = jnp.dot(x, weight[:, columns], preferred_element_type=jnp.float32)
            to_ref[:, :, i * half : (i + 1) * half] = y.reshape(chips, eight, half).astype(
                to_ref.dtype
            )
        to_ref[:, :, 2 * half :] = (
            in_lanes(marks, tokens).reshape(chips, eight, META).astype(to_ref.dtype)
        )


def pair_kernel(keep_ref, got_ref, out_ref):
    out_ref[...] = (keep_ref[...] + got_ref[...].astype(jnp.float32)).astype(out_ref.dtype)


def hidden_kernel(part_ref, out_ref):
    sources = part_ref.shape[0]
    half = out_ref.shape[2]
    both = part_ref[0].astype(jnp.float32)
    for d in range(1, sources):
        both = both + part_ref[d].astype(jnp.float32)
    squares = jnp.sum(both[:, 2 * half :], axis=1, keepdims=True)
    level = lax.rsqrt(squares / D + EPS)
    gate = both[:, :half] * level
    up = both[:, half : 2 * half] * level
    hidden = (gate / (1.0 + jnp.exp(-gate)) * up).astype(jnp.bfloat16)
    out_ref[...] = jnp.broadcast_to(hidden[None], out_ref.shape)


def down(hidden_ref, weight_ref, k):
    half = hidden_ref.shape[2]
    columns = pl.ds(pl.multiple_of(k * half, META), half)
    return lax.dot_general(
        rows_of(hidden_ref[...]),
        weight_ref[:, columns],
        NT,
        preferred_element_type=jnp.float32,
    )


def down_own_kernel(hidden_ref, weight_ref, out_ref):
    out_ref[...] = down(hidden_ref, weight_ref, lax.axis_index("dp") % 2)


def down_kernel(own_ref, hidden_ref, weight_ref, out_ref):
    total = own_ref[...] + down(hidden_ref, weight_ref, 1 - lax.axis_index("dp") % 2)
    out_ref[...] = total.reshape(out_ref.shape).astype(jnp.bfloat16)


def finish_kernel(part_ref, mid_ref, out_ref):
    ffn = part_ref[0].astype(jnp.float32)
    for c in range(1, part_ref.shape[0]):
        ffn = ffn + part_ref[c].astype(jnp.float32)
    out_ref[...] = (mid_ref[...].astype(jnp.float32) + ffn).astype(jnp.bfloat16)


def exchange(x, axis):
    return lax.all_to_all(x, axis, 0, 0)


def exchange_chips(x):
    size = lax.axis_size("dp")
    groups = [list(range(core, size, 2)) for core in range(2)]
    return lax.all_to_all(x, "dp", 0, 0, axis_index_groups=groups)


def other_core(x):
    return lax.ppermute(x, "dp", [(i, i ^ 1) for i in range(lax.axis_size("dp"))])


def on_device(
    stream,
    query,
    new_latent,
    cache,
    cache_scale,
    lengths,
    absorb_value,
    out_proj,
    norm_gain,
    gate_weight,
    up_weight,
    down_weight,
):
    steps, reqs, heads, width = query.shape
    span = cache.shape[1]
    groups = lax.axis_size("ctx")
    holders = lax.axis_size("dp")
    owned = heads // groups
    vhead = absorb_value.shape[2]
    cols = stream.shape[1]
    tokens = stream.shape[0] * groups
    units = gate_weight.shape[1]
    chips = holders // 2
    eight = 2 * steps * reqs
    bf16 = jnp.bfloat16
    f32 = jnp.float32
    smem = pl.BlockSpec(memory_space=pltpu.SMEM)

    cuts = 2
    part = call(
        functools.partial(attend_kernel, sub=512, cuts=cuts),
        jax.ShapeDtypeStruct((groups, reqs * steps * owned + 8, LATENT), bf16),
        [smem] + [pl.BlockSpec(memory_space=pltpu.HBM)] * 4,
        [
            pltpu.VMEM((reqs, width, span), bf16),
            pltpu.VMEM((reqs, steps * heads, span), f32),
            pltpu.VMEM((steps, reqs, width, heads), bf16),
            pltpu.VMEM((steps, reqs, width), bf16),
            pltpu.VMEM((reqs, span), f32),
            pltpu.SemaphoreType.DMA((reqs, cuts)),
            pltpu.SemaphoreType.DMA((3,)),
        ],
        mib=56,
    )(lengths, query.transpose(0, 1, 3, 2), new_latent, cache_scale, cache.transpose(0, 2, 1))
    part = exchange(part, "ctx")

    value = call(
        value_kernel,
        jax.ShapeDtypeStruct((chips, eight, owned * vhead // 2), bf16),
        vmem(2),
        [pltpu.VMEM((reqs, steps * heads, 8 * groups), f32)],
    )(part, absorb_value)
    value = exchange_chips(value)
    other = other_core(value)
    work = pl.CostEstimate(flops=2**29, bytes_accessed=2**20, transcendentals=0)
    attn = call(
        product_kernel,
        jax.ShapeDtypeStruct((cols, chips * eight), f32),
        vmem(2),
        cost=work,
    )(value, out_proj.T)
    attn = call(
        project_kernel,
        jax.ShapeDtypeStruct((groups, cols, tokens), bf16),
        vmem(4),
    )(attn, other, out_proj.T, stream)
    attn = exchange(attn, "ctx")

    block = (chips, tokens // chips, units + META)
    send, keep, mid = call(
        gate_kernel,
        (
            jax.ShapeDtypeStruct(block, bf16),
            jax.ShapeDtypeStruct(block, f32),
            jax.ShapeDtypeStruct(stream.shape, bf16),
        ),
        vmem(4),
        [pltpu.VMEM((tokens, cols), f32)],
    )(attn, norm_gain.reshape(1, cols), gate_weight, up_weight)
    both = call(pair_kernel, jax.ShapeDtypeStruct(block, bf16), vmem(2))(keep, other_core(send))
    both = exchange_chips(both)

    hidden = call(
        hidden_kernel,
        jax.ShapeDtypeStruct((chips, tokens // chips, units // 2), bf16),
        vmem(1),
    )(both)
    hidden = exchange_chips(hidden)

    other = other_core(hidden)
    ffn = call(
        down_own_kernel,
        jax.ShapeDtypeStruct((tokens, cols), f32),
        vmem(2),
        cost=work,
    )(hidden, down_weight.T)
    ffn = call(
        down_kernel,
        jax.ShapeDtypeStruct((groups, tokens // groups, cols), bf16),
        vmem(3),
    )(ffn, other, down_weight.T)
    ffn = exchange(ffn, "ctx")

    return call(finish_kernel, jax.ShapeDtypeStruct(stream.shape, bf16), vmem(2))(ffn, mid)


def solution(mesh):
    return jax.shard_map(
        on_device,
        mesh=mesh,
        in_specs=(
            P("ctx", "dp"),
            P(None, "dp", None, None),
            P(None, "dp", None),
            P("dp", "ctx", None),
            P("dp", "ctx"),
            P("dp"),
            P("ctx", None, None),
            P("ctx", "dp"),
            P("dp"),
            P("dp", "ctx"),
            P("dp", "ctx"),
            P("ctx", "dp"),
        ),
        out_specs=P("ctx", "dp"),
        check_vma=False,
    )
```

```python
import functools

import jax
import jax.numpy as jnp
from jax import lax
from jax.experimental import pallas as pl
from jax.experimental.pallas import tpu as pltpu
from jax.sharding import PartitionSpec as P

D = 7168
LATENT = 512
QKHEAD = 192
EPS = 1e-06

SCORE = QKHEAD ** (-0.5) * 1.4426950408889634
NEG = -1e30
FLOOR = -1e29
META = 128
NT = (((1,), (1,)), ((), ()))


def vmem(n):
    return [pl.BlockSpec(memory_space=pltpu.VMEM)] * n


def call(kernel, out_shape, in_specs, scratch=(), mib=14, cost=None):
    n_out = len(out_shape) if isinstance(out_shape, tuple) else 1
    out_specs = tuple(vmem(n_out)) if isinstance(out_shape, tuple) else vmem(1)[0]
    return pl.pallas_call(
        kernel,
        in_specs=in_specs,
        out_specs=out_specs,
        out_shape=out_shape,
        scratch_shapes=list(scratch),
        compiler_params=pltpu.CompilerParams(vmem_limit_bytes=mib * 2**20),
        cost_estimate=cost,
    )


def pieces(x):
    first = x.astype(jnp.bfloat16).astype(jnp.float32)
    rest = x - first
    second = rest.astype(jnp.bfloat16).astype(jnp.float32)
    return first, second, (rest - second).astype(jnp.bfloat16).astype(jnp.float32)


def in_lanes(columns, rows):
    lane = lax.broadcasted_iota(jnp.int32, (rows, META), 1)
    out = jnp.zeros((rows, META), jnp.float32)
    for i, column in enumerate(columns):
        out = jnp.where(lane == i, column, out)
    return out


def attend_kernel(
    lengths_ref,
    q_hbm,
    new_hbm,
    scale_hbm,
    cache_hbm,
    out_ref,
    keys,
    scores,
    q_ref,
    new_ref,
    scale_ref,
    cache_sems,
    sems,
    *,
    sub,
    cuts,
):
    reqs, width, span = keys.shape
    groups = out_ref.shape[0]
    steps, heads = q_ref.shape[0], q_ref.shape[3]
    rows = steps * heads
    owned = heads // groups
    cut = span // cuts
    ctx_id = lax.axis_index("ctx")
    cache = [
        pltpu.make_async_copy(
            cache_hbm.at[r, :, pl.ds(i * cut, cut)],
            keys.at[r, :, pl.ds(i * cut, cut)],
            cache_sems.at[r, i],
        )
        for r in range(reqs)
        for i in range(cuts)
    ]
    small = [
        pltpu.make_async_copy(q_hbm, q_ref, sems.at[0]),
        pltpu.make_async_copy(new_hbm, new_ref, sems.at[1]),
        pltpu.make_async_copy(scale_hbm, scale_ref, sems.at[2]),
    ]

    left = [lengths_ref[r] - ctx_id * span for r in range(reqs)]
    queries, fresh, new, tops, totals, sums = ([None] * reqs for _ in range(6))
    n = lax.broadcasted_iota(jnp.int32, (META, width), 0)
    col = lax.broadcasted_iota(jnp.int32, (rows, META), 1)
    step = lax.broadcasted_iota(jnp.int32, (rows, META), 0) // heads

    def begin(r):
        queries[r] = jnp.concatenate([q_ref[s, r].T for s in range(steps)], axis=0)
        tokens = jnp.zeros((META, width), jnp.float32)
        for s in range(steps):
            tokens = jnp.where(n == s, new_ref[s, r : r + 1, :].astype(jnp.float32), tokens)
        fresh[r] = tokens.astype(jnp.bfloat16)
        each = lax.dot_general(queries[r], fresh[r], NT, preferred_element_type=jnp.float32)
        new[r] = jnp.where((col <= step) & (ctx_id == 0), each * SCORE, NEG)
        tops[r] = jnp.maximum(new[r], FLOOR)

    def score(r, u):
        part = jnp.dot(queries[r], keys[r, :, u : u + sub], preferred_element_type=jnp.float32)
        ok = lax.broadcasted_iota(jnp.int32, (1, sub), 1) + u < left[r]
        factor = jnp.where(ok, scale_ref[r : r + 1, u : u + sub] * SCORE, 0.0)
        part = part * factor + jnp.where(ok, 0.0, NEG)
        scores[r, :, u : u + sub] = part
        for w in range(0, sub, META):
            tops[r] = jnp.maximum(tops[r], part[:, w : w + META])

    def top(r):
        tops[r] = jnp.max(tops[r], axis=1, keepdims=True)
        totals[r] = jnp.exp2(new[r] - tops[r])
        sums[r] = jnp.dot(
            totals[r].astype(jnp.bfloat16),
            fresh[r][:, :LATENT],
            preferred_element_type=jnp.float32,
        )

    def weigh(r, u):
        probs = jnp.exp2(scores[r, :, u : u + sub] - tops[r])
        for w in range(0, sub, META):
            totals[r] = totals[r] + probs[:, w : w + META]
        probs = (probs * scale_ref[r : r + 1, u : u + sub]).astype(jnp.bfloat16)
        sums[r] = sums[r] + lax.dot_general(
            probs, keys[r, 0:LATENT, u : u + sub], NT, preferred_element_type=jnp.float32
        )

    def write(r):
        acc = sums[r].astype(jnp.bfloat16)
        total = jnp.sum(totals[r], axis=1, keepdims=True)
        meta = in_lanes(pieces(tops[r]) + pieces(total), rows).T[:8].astype(jnp.bfloat16)
        for g in range(groups):
            for s in range(steps):
                at = s * heads + g * owned
                to = (r * steps + s) * owned
                out_ref[g, to : to + owned, :] = acc[at : at + owned]
            out_ref[g, reqs * steps * owned :, r * rows : (r + 1) * rows] = meta

    def attend(active):
        order = [r * cuts + i for r in active for i in range(cuts)]
        small[0].start()
        cache[order[0]].start()
        small[1].start()
        small[2].start()
        cache[order[1]].start()
        for copy in small:
            copy.wait()
        for r in active:
            begin(r)
        for n in range(len(active) + 1):
            for u in range(0, span, sub):
                if n < len(active):
                    if u % cut == 0:
                        at = n * cuts + u // cut
                        cache[order[at]].wait()
                        if at + 2 < len(order):
                            cache[order[at + 2]].start()
                    score(active[n], u)
                if n > 0:
                    weigh(active[n - 1], u)
            if n > 0:
                write(active[n - 1])
            if n < len(active):
                top(active[n])
        for r in range(reqs):
            if r not in active:
                skip(r)

    def skip(r):
        tops[r] = jnp.full((rows, 1), FLOOR, jnp.float32)
        totals[r] = jnp.zeros((rows, 1), jnp.float32)
        sums[r] = jnp.zeros((rows, LATENT), jnp.float32)
        write(r)

    first, second = (left[r] > 0 for r in range(reqs))

    @pl.when(first & second)
    def _():
        attend([0, 1])

    @pl.when(first & ~second)
    def _():
        attend([0])

    @pl.when(second & ~first)
    def _():
        attend([1])

    @pl.when(~first & ~second)
    def _():
        for r in range(reqs):
            skip(r)


def value_kernel(part_ref, absorb_ref, out_ref, marks):
    sources = part_ref.shape[0]
    owned, _, vhead = absorb_ref.shape
    reqs, all_rows, _ = marks.shape
    rows = part_ref.shape[1] - 8
    tokens = rows // owned
    steps = tokens // reqs
    heads = all_rows // steps
    half = owned // 2
    at = lax.axis_index("ctx") * owned
    found = []
    for r in range(reqs):
        meta = [part_ref[c, rows:, r * all_rows : (r + 1) * all_rows] for c in range(sources)]
        meta = jnp.concatenate([m.astype(jnp.float32) for m in meta], axis=0)
        marks[r] = meta.T
        for s in range(steps):
            found.append(marks[r, pl.ds(pl.multiple_of(s * heads + at, owned), owned), :])
    found = jnp.concatenate(found, axis=0)
    tops, totals = [], []
    for c in range(sources):
        i = 8 * c
        tops.append(found[:, i : i + 1] + found[:, i + 1 : i + 2] + found[:, i + 2 : i + 3])
        totals.append(found[:, i + 3 : i + 4] + found[:, i + 4 : i + 5] + found[:, i + 5 : i + 6])
    top = functools.reduce(jnp.maximum, tops)
    total = jnp.zeros_like(top)
    acc = jnp.zeros((rows, LATENT), jnp.float32)
    for c in range(sources):
        factor = jnp.exp2(tops[c] - top)
        total = total + totals[c] * factor
        acc = acc + part_ref[c, :rows, :].astype(jnp.float32) * factor
    attended = (acc / total).astype(jnp.bfloat16)
    sides = []
    for side in range(2):
        cols = []
        for h in range(side * half, (side + 1) * half):
            each = jnp.dot(attended, absorb_ref[h], preferred_element_type=jnp.float32)
            cols.append(each.reshape(tokens, owned, vhead)[:, h, :])
        sides.append(jnp.concatenate(cols, axis=1))
    value = jnp.concatenate(sides, axis=0).astype(jnp.bfloat16)
    out_ref[...] = jnp.broadcast_to(value[None], out_ref.shape)


def rows_of(x):
    x = x.astype(jnp.float32)
    return x.reshape(x.shape[0] * x.shape[1], x.shape[2]).astype(jnp.bfloat16)


def product(value_ref, weight_ref):
    x = rows_of(value_ref[...])
    half = x.shape[1]
    low = lax.dot_general(weight_ref[:, :half], x, NT, preferred_element_type=jnp.float32)
    high = lax.dot_general(weight_ref[:, half:], x, NT, preferred_element_type=jnp.float32)
    return low + pltpu.roll(high, x.shape[0] - 4, 1)


def product_kernel(value_ref, weight_ref, out_ref):
    out_ref[...] = product(value_ref, weight_ref)


def project_kernel(own_ref, value_ref, weight_ref, stream_ref, out_ref):
    copies, cols, tokens = out_ref.shape
    owned = stream_ref.shape[0]
    per = tokens // 2
    width = 2 * own_ref.shape[1]
    core = lax.axis_index("dp") % 2

    def place(t):
        t_in = jnp.where(t >= per, t - per, t)
        d = t_in // 2
        first = jnp.where(d % 2 == core, 0, width // 2) + 8 * (d // 2)
        return first + 2 * (t_in % 2) + jnp.where(t >= per, 1, 0)

    def one_hot(shape, token_dim, offset):
        t = lax.broadcasted_iota(jnp.int32, shape, token_dim) + offset
        k = lax.broadcasted_iota(jnp.int32, shape, 1 - token_dim)
        return jnp.where(k == place(t), 1.0, 0.0).astype(jnp.bfloat16)

    both = jnp.concatenate([own_ref[...], product(value_ref, weight_ref)], axis=1)
    mine = one_hot((owned, width), 0, lax.axis_index("ctx") * owned)
    both = both + lax.dot_general(
        stream_ref[...], mine, (((0,), (0,)), ((), ())), preferred_element_type=jnp.float32
    )
    ordered = jnp.dot(
        both.astype(jnp.bfloat16),
        one_hot((width, tokens), 1, 0),
        preferred_element_type=jnp.float32,
    ).astype(jnp.bfloat16)
    out_ref[...] = jnp.broadcast_to(ordered[None], out_ref.shape)


def gate_products(x, gate_ref, up_ref, k, marks, to_ref):
    chips, eight, _ = to_ref.shape
    half = gate_ref.shape[1] // 2
    columns = pl.ds(pl.multiple_of(k * half, META), half)
    for i, weight in enumerate((gate_ref, up_ref)):
        y = jnp.dot(x, weight[:, columns], preferred_element_type=jnp.float32)
        to_ref[:, :, i * half : (i + 1) * half] = y.reshape(chips, eight, half).astype(to_ref.dtype)
    to_ref[:, :, 2 * half :] = marks.reshape(chips, eight, META).astype(to_ref.dtype)


def gate_kernel(
    part_ref, gain_ref, gate_ref, up_ref, send_ref, x_ref, marks_ref, mid_ref, whole
):
    sources, cols, tokens = part_ref.shape
    owned = mid_ref.shape[0]
    mid = part_ref[0].astype(jnp.float32)
    for c in range(1, sources):
        mid = mid + part_ref[c].astype(jnp.float32)
    mid = mid.astype(jnp.bfloat16).astype(jnp.float32).T
    whole[...] = mid
    at = pl.multiple_of(lax.axis_index("ctx") * owned, owned)
    mid_ref[...] = whole[pl.ds(at, owned), :].astype(jnp.bfloat16)
    squares = pieces(jnp.sum(mid * mid, axis=1, keepdims=True))
    none = (jnp.zeros_like(squares[0]),) * 3
    x = (mid * gain_ref[...].astype(jnp.float32)).astype(jnp.bfloat16)
    x_ref[...] = x
    marks_ref[...] = in_lanes(none + squares, tokens)
    core = lax.axis_index("dp") % 2
    gate_products(x, gate_ref, up_ref, 1 - core, in_lanes(squares, tokens), send_ref)


def gate_own_kernel(x_ref, marks_ref, gate_ref, up_ref, keep_ref):
    core = lax.axis_index("dp") % 2
    gate_products(x_ref[...], gate_ref, up_ref, core, marks_ref[...], keep_ref)


def pair_kernel(keep_ref, got_ref, out_ref):
    out_ref[...] = (keep_ref[...] + got_ref[...].astype(jnp.float32)).astype(out_ref.dtype)


def hidden_kernel(part_ref, out_ref):
    sources = part_ref.shape[0]
    half = out_ref.shape[2]
    both = part_ref[0].astype(jnp.float32)
    for d in range(1, sources):
        both = both + part_ref[d].astype(jnp.float32)
    squares = jnp.sum(both[:, 2 * half :], axis=1, keepdims=True)
    level = lax.rsqrt(squares / D + EPS)
    gate = both[:, :half] * level
    up = both[:, half : 2 * half] * level
    hidden = (gate / (1.0 + jnp.exp(-gate)) * up).astype(jnp.bfloat16)
    out_ref[...] = jnp.broadcast_to(hidden[None], out_ref.shape)


def down(hidden_ref, weight_ref, k):
    half = hidden_ref.shape[2]
    columns = pl.ds(pl.multiple_of(k * half, META), half)
    return lax.dot_general(
        rows_of(hidden_ref[...]),
        weight_ref[:, columns],
        NT,
        preferred_element_type=jnp.float32,
    )


def down_own_kernel(hidden_ref, weight_ref, out_ref):
    out_ref[...] = down(hidden_ref, weight_ref, lax.axis_index("dp") % 2)


def down_kernel(own_ref, hidden_ref, weight_ref, out_ref):
    total = own_ref[...] + down(hidden_ref, weight_ref, 1 - lax.axis_index("dp") % 2)
    out_ref[...] = total.reshape(out_ref.shape).astype(jnp.bfloat16)


def finish_kernel(part_ref, mid_ref, out_ref):
    ffn = part_ref[0].astype(jnp.float32)
    for c in range(1, part_ref.shape[0]):
        ffn = ffn + part_ref[c].astype(jnp.float32)
    out_ref[...] = (mid_ref[...].astype(jnp.float32) + ffn).astype(jnp.bfloat16)


def exchange(x, axis):
    return lax.all_to_all(x, axis, 0, 0)


def exchange_chips(x):
    size = lax.axis_size("dp")
    groups = [list(range(core, size, 2)) for core in range(2)]
    return lax.all_to_all(x, "dp", 0, 0, axis_index_groups=groups)


def other_core(x):
    return lax.ppermute(x, "dp", [(i, i ^ 1) for i in range(lax.axis_size("dp"))])


def on_device(
    stream,
    query,
    new_latent,
    cache,
    cache_scale,
    lengths,
    absorb_value,
    out_proj,
    norm_gain,
    gate_weight,
    up_weight,
    down_weight,
):
    steps, reqs, heads, width = query.shape
    span = cache.shape[1]
    groups = lax.axis_size("ctx")
    holders = lax.axis_size("dp")
    owned = heads // groups
    vhead = absorb_value.shape[2]
    cols = stream.shape[1]
    tokens = stream.shape[0] * groups
    units = gate_weight.shape[1]
    chips = holders // 2
    eight = 2 * steps * reqs
    bf16 = jnp.bfloat16
    f32 = jnp.float32
    smem = pl.BlockSpec(memory_space=pltpu.SMEM)

    cuts = 2
    part = call(
        functools.partial(attend_kernel, sub=512, cuts=cuts),
        jax.ShapeDtypeStruct((groups, reqs * steps * owned + 8, LATENT), bf16),
        [smem] + [pl.BlockSpec(memory_space=pltpu.HBM)] * 4,
        [
            pltpu.VMEM((reqs, width, span), bf16),
            pltpu.VMEM((reqs, steps * heads, span), f32),
            pltpu.VMEM((steps, reqs, width, heads), bf16),
            pltpu.VMEM((steps, reqs, width), bf16),
            pltpu.VMEM((reqs, span), f32),
            pltpu.SemaphoreType.DMA((reqs, cuts)),
            pltpu.SemaphoreType.DMA((3,)),
        ],
        mib=56,
    )(lengths, query.transpose(0, 1, 3, 2), new_latent, cache_scale, cache.transpose(0, 2, 1))
    part = exchange(part, "ctx")

    value = call(
        value_kernel,
        jax.ShapeDtypeStruct((chips, eight, owned * vhead // 2), bf16),
        vmem(2),
        [pltpu.VMEM((reqs, steps * heads, 8 * groups), f32)],
    )(part, absorb_value)
    value = exchange_chips(value)
    other = other_core(value)
    work = pl.CostEstimate(flops=2**29, bytes_accessed=2**20, transcendentals=0)
    attn = call(
        product_kernel,
        jax.ShapeDtypeStruct((cols, chips * eight), f32),
        vmem(2),
        cost=work,
    )(value, out_proj.T)
    attn = call(
        project_kernel,
        jax.ShapeDtypeStruct((groups, cols, tokens), bf16),
        vmem(4),
    )(attn, other, out_proj.T, stream)
    attn, gain = lax.optimization_barrier((attn, norm_gain.reshape(1, cols)))
    attn = exchange(attn, "ctx")

    block = (chips, tokens // chips, units + META)
    send, x, marks, mid = call(
        gate_kernel,
        (
            jax.ShapeDtypeStruct(block, bf16),
            jax.ShapeDtypeStruct((tokens, cols), bf16),
            jax.ShapeDtypeStruct((tokens, META), f32),
            jax.ShapeDtypeStruct(stream.shape, bf16),
        ),
        vmem(4),
        [pltpu.VMEM((tokens, cols), f32)],
    )(attn, gain, gate_weight, up_weight)
    got = other_core(send)
    keep = call(gate_own_kernel, jax.ShapeDtypeStruct(block, f32), vmem(4), cost=work)(
        x, marks, gate_weight, up_weight
    )
    both = call(pair_kernel, jax.ShapeDtypeStruct(block, bf16), vmem(2))(keep, got)
    both = exchange_chips(both)

    hidden = call(
        hidden_kernel,
        jax.ShapeDtypeStruct((chips, tokens // chips, units // 2), bf16),
        vmem(1),
    )(both)
    hidden = exchange_chips(hidden)

    other = other_core(hidden)
    ffn = call(
        down_own_kernel,
        jax.ShapeDtypeStruct((tokens, cols), f32),
        vmem(2),
        cost=work,
    )(hidden, down_weight.T)
    ffn = call(
        down_kernel,
        jax.ShapeDtypeStruct((groups, tokens // groups, cols), bf16),
        vmem(3),
    )(ffn, other, down_weight.T)
    ffn = exchange(ffn, "ctx")

    return call(finish_kernel, jax.ShapeDtypeStruct(stream.shape, bf16), vmem(2))(ffn, mid)


def solution(mesh):
    return jax.shard_map(
        on_device,
        mesh=mesh,
        in_specs=(
            P("ctx", "dp"),
            P(None, "dp", None, None),
            P(None, "dp", None),
            P("dp", "ctx", None),
            P("dp", "ctx"),
            P("dp"),
            P("ctx", None, None),
            P("ctx", "dp"),
            P("dp"),
            P("dp", "ctx"),
            P("dp", "ctx"),
            P("ctx", "dp"),
        ),
        out_specs=P("ctx", "dp"),
        check_vma=False,
    )
```

```python
import functools

import jax
import jax.numpy as jnp
from jax import lax
from jax.experimental import pallas as pl
from jax.experimental.pallas import tpu as pltpu
from jax.sharding import PartitionSpec as P

D = 7168
LATENT = 512
QKHEAD = 192
EPS = 1e-06

SCORE = QKHEAD ** (-0.5) * 1.4426950408889634
NEG = -1e30
FLOOR = -1e29
META = 128
NT = (((1,), (1,)), ((), ()))


def vmem(n):
    return [pl.BlockSpec(memory_space=pltpu.VMEM)] * n


def call(kernel, out_shape, in_specs, scratch=(), mib=14, cost=None, out_specs=None):
    n_out = len(out_shape) if isinstance(out_shape, tuple) else 1
    if out_specs is None:
        out_specs = tuple(vmem(n_out)) if isinstance(out_shape, tuple) else vmem(1)[0]
    return pl.pallas_call(
        kernel,
        in_specs=in_specs,
        out_specs=out_specs,
        out_shape=out_shape,
        scratch_shapes=list(scratch),
        compiler_params=pltpu.CompilerParams(vmem_limit_bytes=mib * 2**20),
        cost_estimate=cost,
    )


def pieces(x):
    first = x.astype(jnp.bfloat16).astype(jnp.float32)
    rest = x - first
    second = rest.astype(jnp.bfloat16).astype(jnp.float32)
    return first, second, (rest - second).astype(jnp.bfloat16).astype(jnp.float32)


def in_lanes(columns, rows):
    lane = lax.broadcasted_iota(jnp.int32, (rows, META), 1)
    out = jnp.zeros((rows, META), jnp.float32)
    for i, column in enumerate(columns):
        out = jnp.where(lane == i, column, out)
    return out


def attend_kernel(
    lengths_ref,
    q_hbm,
    new_hbm,
    scale_hbm,
    cache_hbm,
    out_hbm,
    out_ref,
    keys,
    scores,
    q_ref,
    new_ref,
    scale_ref,
    cache_sems,
    sems,
    out_sems,
    *,
    sub,
    cuts,
):
    reqs, width, span = keys.shape
    groups = out_ref.shape[0]
    steps, heads = q_ref.shape[0], q_ref.shape[3]
    rows = steps * heads
    owned = heads // groups
    cut = span // cuts
    ctx_id = lax.axis_index("ctx")
    cache = [
        pltpu.make_async_copy(
            cache_hbm.at[r, :, pl.ds(i * cut, cut)],
            keys.at[r, :, pl.ds(i * cut, cut)],
            cache_sems.at[r, i],
        )
        for r in range(reqs)
        for i in range(cuts)
    ]
    small = [
        pltpu.make_async_copy(q_hbm, q_ref, sems.at[0]),
        pltpu.make_async_copy(new_hbm, new_ref, sems.at[1]),
        pltpu.make_async_copy(scale_hbm, scale_ref, sems.at[2]),
    ]

    early = steps * owned
    rest = out_ref.shape[1] - early
    leave = [
        pltpu.make_async_copy(
            out_ref.at[:, pl.ds(at, size), :], out_hbm.at[:, pl.ds(at, size), :], out_sems.at[i]
        )
        for i, (at, size) in enumerate(((0, early), (early, rest)))
    ]
    left = [lengths_ref[r] - ctx_id * span for r in range(reqs)]
    queries, fresh, new, tops, totals, sums = ([None] * reqs for _ in range(6))
    n = lax.broadcasted_iota(jnp.int32, (META, width), 0)
    col = lax.broadcasted_iota(jnp.int32, (rows, META), 1)
    step = lax.broadcasted_iota(jnp.int32, (rows, META), 0) // heads

    def begin(r):
        queries[r] = jnp.concatenate([q_ref[s, r].T for s in range(steps)], axis=0)
        tokens = jnp.zeros((META, width), jnp.float32)
        for s in range(steps):
            tokens = jnp.where(n == s, new_ref[s, r : r + 1, :].astype(jnp.float32), tokens)
        fresh[r] = tokens.astype(jnp.bfloat16)
        each = lax.dot_general(queries[r], fresh[r], NT, preferred_element_type=jnp.float32)
        new[r] = jnp.where((col <= step) & (ctx_id == 0), each * SCORE, NEG)
        tops[r] = jnp.maximum(new[r], FLOOR)

    def score(r, u):
        part = jnp.dot(queries[r], keys[r, :, u : u + sub], preferred_element_type=jnp.float32)
        ok = lax.broadcasted_iota(jnp.int32, (1, sub), 1) + u < left[r]
        factor = jnp.where(ok, scale_ref[r : r + 1, u : u + sub] * SCORE, 0.0)
        part = part * factor + jnp.where(ok, 0.0, NEG)
        scores[r, :, u : u + sub] = part
        for w in range(0, sub, META):
            tops[r] = jnp.maximum(tops[r], part[:, w : w + META])

    def top(r):
        tops[r] = jnp.max(tops[r], axis=1, keepdims=True)
        totals[r] = jnp.exp2(new[r] - tops[r])
        sums[r] = jnp.dot(
            totals[r].astype(jnp.bfloat16),
            fresh[r][:, :LATENT],
            preferred_element_type=jnp.float32,
        )

    def weigh(r, u):
        probs = jnp.exp2(scores[r, :, u : u + sub] - tops[r])
        for w in range(0, sub, META):
            totals[r] = totals[r] + probs[:, w : w + META]
        probs = (probs * scale_ref[r : r + 1, u : u + sub]).astype(jnp.bfloat16)
        sums[r] = sums[r] + lax.dot_general(
            probs, keys[r, 0:LATENT, u : u + sub], NT, preferred_element_type=jnp.float32
        )

    def write(r):
        acc = sums[r].astype(jnp.bfloat16)
        total = jnp.sum(totals[r], axis=1, keepdims=True)
        meta = in_lanes(pieces(tops[r]) + pieces(total), rows).T[:8].astype(jnp.bfloat16)
        for g in range(groups):
            for s in range(steps):
                at = s * heads + g * owned
                to = (r * steps + s) * owned
                out_ref[g, to : to + owned, :] = acc[at : at + owned]
            out_ref[g, reqs * steps * owned :, r * rows : (r + 1) * rows] = meta

    def attend(active):
        order = [r * cuts + i for r in active for i in range(cuts)]
        small[0].start()
        cache[order[0]].start()
        small[1].start()
        small[2].start()
        cache[order[1]].start()
        for copy in small:
            copy.wait()
        for r in active:
            begin(r)
        for n in range(len(active) + 1):
            for u in range(0, span, sub):
                if n < len(active):
                    if u % cut == 0:
                        at = n * cuts + u // cut
                        cache[order[at]].wait()
                        if at + 2 < len(order):
                            cache[order[at + 2]].start()
                    score(active[n], u)
                if n > 0:
                    weigh(active[n - 1], u)
            if n > 0:
                write(active[n - 1])
            if n == 1 and len(active) == reqs:
                leave[0].start()
            if n < len(active):
                top(active[n])
        for r in range(reqs):
            if r not in active:
                skip(r)
        finish(len(active) < reqs)

    def skip(r):
        tops[r] = jnp.full((rows, 1), FLOOR, jnp.float32)
        totals[r] = jnp.zeros((rows, 1), jnp.float32)
        sums[r] = jnp.zeros((rows, LATENT), jnp.float32)
        write(r)

    def finish(whole):
        if whole:
            leave[0].start()
        leave[1].start()
        for copy in leave:
            copy.wait()

    first, second = (left[r] > 0 for r in range(reqs))

    @pl.when(first & second)
    def _():
        attend([0, 1])

    @pl.when(first & ~second)
    def _():
        attend([0])

    @pl.when(second & ~first)
    def _():
        attend([1])

    @pl.when(~first & ~second)
    def _():
        for r in range(reqs):
            skip(r)
        finish(True)


def value_kernel(part_ref, absorb_ref, out_ref, marks):
    sources = part_ref.shape[0]
    owned, _, vhead = absorb_ref.shape
    reqs, all_rows, _ = marks.shape
    rows = part_ref.shape[1] - 8
    tokens = rows // owned
    steps = tokens // reqs
    heads = all_rows // steps
    half = owned // 2
    at = lax.axis_index("ctx") * owned
    found = []
    for r in range(reqs):
        meta = [part_ref[c, rows:, r * all_rows : (r + 1) * all_rows] for c in range(sources)]
        meta = jnp.concatenate([m.astype(jnp.float32) for m in meta], axis=0)
        marks[r] = meta.T
        for s in range(steps):
            found.append(marks[r, pl.ds(pl.multiple_of(s * heads + at, owned), owned), :])
    found = jnp.concatenate(found, axis=0)
    tops, totals = [], []
    for c in range(sources):
        i = 8 * c
        tops.append(found[:, i : i + 1] + found[:, i + 1 : i + 2] + found[:, i + 2 : i + 3])
        totals.append(found[:, i + 3 : i + 4] + found[:, i + 4 : i + 5] + found[:, i + 5 : i + 6])
    top = functools.reduce(jnp.maximum, tops)
    total = jnp.zeros_like(top)
    acc = jnp.zeros((rows, LATENT), jnp.float32)
    for c in range(sources):
        factor = jnp.exp2(tops[c] - top)
        total = total + totals[c] * factor
        acc = acc + part_ref[c, :rows, :].astype(jnp.float32) * factor
    attended = (acc / total).astype(jnp.bfloat16)
    sides = []
    for side in range(2):
        cols = []
        for h in range(side * half, (side + 1) * half):
            each = jnp.dot(attended, absorb_ref[h], preferred_element_type=jnp.float32)
            cols.append(each.reshape(tokens, owned, vhead)[:, h, :])
        sides.append(jnp.concatenate(cols, axis=1))
    value = jnp.concatenate(sides, axis=0).astype(jnp.bfloat16)
    out_ref[...] = jnp.broadcast_to(value[None], out_ref.shape)


def rows_of(x):
    x = x.astype(jnp.float32)
    return x.reshape(x.shape[0] * x.shape[1], x.shape[2]).astype(jnp.bfloat16)


def product(value_ref, weight_ref):
    x = rows_of(value_ref[...])
    half = x.shape[1]
    low = lax.dot_general(weight_ref[:, :half], x, NT, preferred_element_type=jnp.float32)
    high = lax.dot_general(weight_ref[:, half:], x, NT, preferred_element_type=jnp.float32)
    return low + pltpu.roll(high, x.shape[0] - 4, 1)


def product_kernel(value_ref, weight_ref, out_ref):
    out_ref[...] = product(value_ref, weight_ref)


def project_kernel(own_ref, value_ref, weight_ref, stream_ref, out_ref):
    copies, cols, tokens = out_ref.shape
    owned = stream_ref.shape[0]
    per = tokens // 2
    width = 2 * own_ref.shape[1]
    core = lax.axis_index("dp") % 2

    def place(t):
        t_in = jnp.where(t >= per, t - per, t)
        d = t_in // 2
        first = jnp.where(d % 2 == core, 0, width // 2) + 8 * (d // 2)
        return first + 2 * (t_in % 2) + jnp.where(t >= per, 1, 0)

    def one_hot(shape, token_dim, offset):
        t = lax.broadcasted_iota(jnp.int32, shape, token_dim) + offset
        k = lax.broadcasted_iota(jnp.int32, shape, 1 - token_dim)
        return jnp.where(k == place(t), 1.0, 0.0).astype(jnp.bfloat16)

    both = jnp.concatenate([own_ref[...], product(value_ref, weight_ref)], axis=1)
    mine = one_hot((owned, width), 0, lax.axis_index("ctx") * owned)
    both = both + lax.dot_general(
        stream_ref[...], mine, (((0,), (0,)), ((), ())), preferred_element_type=jnp.float32
    )
    ordered = jnp.dot(
        both.astype(jnp.bfloat16),
        one_hot((width, tokens), 1, 0),
        preferred_element_type=jnp.float32,
    ).astype(jnp.bfloat16)
    out_ref[...] = jnp.broadcast_to(ordered[None], out_ref.shape)


def gate_products(x, gate_ref, up_ref, k, marks, to_ref):
    chips, eight, _ = to_ref.shape
    half = gate_ref.shape[1] // 2
    columns = pl.ds(pl.multiple_of(k * half, META), half)
    for i, weight in enumerate((gate_ref, up_ref)):
        y = jnp.dot(x, weight[:, columns], preferred_element_type=jnp.float32)
        to_ref[:, :, i * half : (i + 1) * half] = y.reshape(chips, eight, half).astype(to_ref.dtype)
    to_ref[:, :, 2 * half :] = marks.reshape(chips, eight, META).astype(to_ref.dtype)


def gate_kernel(
    part_ref, gain_ref, gate_ref, up_ref, send_ref, x_ref, marks_ref, mid_ref, whole
):
    sources, cols, tokens = part_ref.shape
    owned = mid_ref.shape[0]
    mid = part_ref[0].astype(jnp.float32)
    for c in range(1, sources):
        mid = mid + part_ref[c].astype(jnp.float32)
    mid = mid.astype(jnp.bfloat16).astype(jnp.float32).T
    whole[...] = mid
    at = pl.multiple_of(lax.axis_index("ctx") * owned, owned)
    mid_ref[...] = whole[pl.ds(at, owned), :].astype(jnp.bfloat16)
    squares = pieces(jnp.sum(mid * mid, axis=1, keepdims=True))
    none = (jnp.zeros_like(squares[0]),) * 3
    x = (mid * gain_ref[...].astype(jnp.float32)).astype(jnp.bfloat16)
    x_ref[...] = x
    marks_ref[...] = in_lanes(none + squares, tokens)
    core = lax.axis_index("dp") % 2
    gate_products(x, gate_ref, up_ref, 1 - core, in_lanes(squares, tokens), send_ref)


def gate_own_kernel(x_ref, marks_ref, gate_ref, up_ref, keep_ref):
    core = lax.axis_index("dp") % 2
    gate_products(x_ref[...], gate_ref, up_ref, core, marks_ref[...], keep_ref)


def pair_kernel(keep_ref, got_ref, out_ref):
    out_ref[...] = (keep_ref[...] + got_ref[...].astype(jnp.float32)).astype(out_ref.dtype)


def hidden_kernel(part_ref, out_ref):
    sources = part_ref.shape[0]
    half = out_ref.shape[2]
    both = part_ref[0].astype(jnp.float32)
    for d in range(1, sources):
        both = both + part_ref[d].astype(jnp.float32)
    squares = jnp.sum(both[:, 2 * half :], axis=1, keepdims=True)
    level = lax.rsqrt(squares / D + EPS)
    gate = both[:, :half] * level
    up = both[:, half : 2 * half] * level
    hidden = (gate / (1.0 + jnp.exp(-gate)) * up).astype(jnp.bfloat16)
    out_ref[...] = jnp.broadcast_to(hidden[None], out_ref.shape)


def down(hidden_ref, weight_ref, k):
    half = hidden_ref.shape[2]
    columns = pl.ds(pl.multiple_of(k * half, META), half)
    return lax.dot_general(
        rows_of(hidden_ref[...]),
        weight_ref[:, columns],
        NT,
        preferred_element_type=jnp.float32,
    )


def down_own_kernel(hidden_ref, weight_ref, out_ref):
    out_ref[...] = down(hidden_ref, weight_ref, lax.axis_index("dp") % 2)


def down_kernel(own_ref, hidden_ref, weight_ref, out_ref):
    total = own_ref[...] + down(hidden_ref, weight_ref, 1 - lax.axis_index("dp") % 2)
    out_ref[...] = total.reshape(out_ref.shape).astype(jnp.bfloat16)


def finish_kernel(part_ref, mid_ref, out_ref):
    ffn = part_ref[0].astype(jnp.float32)
    for c in range(1, part_ref.shape[0]):
        ffn = ffn + part_ref[c].astype(jnp.float32)
    out_ref[...] = (mid_ref[...].astype(jnp.float32) + ffn).astype(jnp.bfloat16)


def exchange(x, axis):
    return lax.all_to_all(x, axis, 0, 0)


def exchange_chips(x):
    size = lax.axis_size("dp")
    groups = [list(range(core, size, 2)) for core in range(2)]
    return lax.all_to_all(x, "dp", 0, 0, axis_index_groups=groups)


def other_core(x):
    return lax.ppermute(x, "dp", [(i, i ^ 1) for i in range(lax.axis_size("dp"))])


def on_device(
    stream,
    query,
    new_latent,
    cache,
    cache_scale,
    lengths,
    absorb_value,
    out_proj,
    norm_gain,
    gate_weight,
    up_weight,
    down_weight,
):
    steps, reqs, heads, width = query.shape
    span = cache.shape[1]
    groups = lax.axis_size("ctx")
    holders = lax.axis_size("dp")
    owned = heads // groups
    vhead = absorb_value.shape[2]
    cols = stream.shape[1]
    tokens = stream.shape[0] * groups
    units = gate_weight.shape[1]
    chips = holders // 2
    eight = 2 * steps * reqs
    bf16 = jnp.bfloat16
    f32 = jnp.float32
    smem = pl.BlockSpec(memory_space=pltpu.SMEM)

    cuts = 2
    part = call(
        functools.partial(attend_kernel, sub=512, cuts=cuts),
        jax.ShapeDtypeStruct((groups, reqs * steps * owned + 8, LATENT), bf16),
        [smem] + [pl.BlockSpec(memory_space=pltpu.HBM)] * 4,
        [
            pltpu.VMEM((groups, reqs * steps * owned + 8, LATENT), bf16),
            pltpu.VMEM((reqs, width, span), bf16),
            pltpu.VMEM((reqs, steps * heads, span), f32),
            pltpu.VMEM((steps, reqs, width, heads), bf16),
            pltpu.VMEM((steps, reqs, width), bf16),
            pltpu.VMEM((reqs, span), f32),
            pltpu.SemaphoreType.DMA((reqs, cuts)),
            pltpu.SemaphoreType.DMA((3,)),
            pltpu.SemaphoreType.DMA((2,)),
        ],
        mib=56,
        out_specs=pl.BlockSpec(memory_space=pltpu.HBM),
    )(lengths, query.transpose(0, 1, 3, 2), new_latent, cache_scale, cache.transpose(0, 2, 1))
    part = exchange(part, "ctx")

    value = call(
        value_kernel,
        jax.ShapeDtypeStruct((chips, eight, owned * vhead // 2), bf16),
        vmem(2),
        [pltpu.VMEM((reqs, steps * heads, 8 * groups), f32)],
    )(part, absorb_value)
    value = exchange_chips(value)
    other = other_core(value)
    work = pl.CostEstimate(flops=2**29, bytes_accessed=2**20, transcendentals=0)
    attn = call(
        product_kernel,
        jax.ShapeDtypeStruct((cols, chips * eight), f32),
        vmem(2),
        cost=work,
    )(value, out_proj.T)
    attn = call(
        project_kernel,
        jax.ShapeDtypeStruct((groups, cols, tokens), bf16),
        vmem(4),
    )(attn, other, out_proj.T, stream)
    attn, gain = lax.optimization_barrier((attn, norm_gain.reshape(1, cols)))
    attn = exchange(attn, "ctx")

    block = (chips, tokens // chips, units + META)
    send, x, marks, mid = call(
        gate_kernel,
        (
            jax.ShapeDtypeStruct(block, bf16),
            jax.ShapeDtypeStruct((tokens, cols), bf16),
            jax.ShapeDtypeStruct((tokens, META), f32),
            jax.ShapeDtypeStruct(stream.shape, bf16),
        ),
        vmem(4),
        [pltpu.VMEM((tokens, cols), f32)],
    )(attn, gain, gate_weight, up_weight)
    got = other_core(send)
    keep = call(gate_own_kernel, jax.ShapeDtypeStruct(block, f32), vmem(4), cost=work)(
        x, marks, gate_weight, up_weight
    )
    both = call(pair_kernel, jax.ShapeDtypeStruct(block, bf16), vmem(2))(keep, got)
    both = exchange_chips(both)

    hidden = call(
        hidden_kernel,
        jax.ShapeDtypeStruct((chips, tokens // chips, units // 2), bf16),
        vmem(1),
    )(both)
    hidden = exchange_chips(hidden)

    other = other_core(hidden)
    ffn = call(
        down_own_kernel,
        jax.ShapeDtypeStruct((tokens, cols), f32),
        vmem(2),
        cost=work,
    )(hidden, down_weight.T)
    ffn = call(
        down_kernel,
        jax.ShapeDtypeStruct((groups, tokens // groups, cols), bf16),
        vmem(3),
    )(ffn, other, down_weight.T)
    ffn = exchange(ffn, "ctx")

    return call(finish_kernel, jax.ShapeDtypeStruct(stream.shape, bf16), vmem(2))(ffn, mid)


def solution(mesh):
    return jax.shard_map(
        on_device,
        mesh=mesh,
        in_specs=(
            P("ctx", "dp"),
            P(None, "dp", None, None),
            P(None, "dp", None),
            P("dp", "ctx", None),
            P("dp", "ctx"),
            P("dp"),
            P("ctx", None, None),
            P("ctx", "dp"),
            P("dp"),
            P("dp", "ctx"),
            P("dp", "ctx"),
            P("ctx", "dp"),
        ),
        out_specs=P("ctx", "dp"),
        check_vma=False,
    )
```
